32 devices in a mesh: rep: 2 (over y), gx: 4 (over z), gy: 2 (over x), gz: 2 (over core).
Axes of the slice: x: 2, y: 2, z: 4, core: 2. Of those that a mesh axis runs over, the one named last changes fastest.
Arguments:
- positions: float32 [3, 16, 4, 128], P(None, ('rep', 'gx'), 'gy', 'gz'), parts along dimension 1, may hold values from 0 to 6
- features: float32 [64, 16, 4, 128], P(None, ('rep', 'gx'), 'gy', 'gz'), parts along dimension 1, may hold values from -6 to 6
- nbr_index: int32 [48, 16, 4, 128], P(None, ('rep', 'gx'), 'gy', 'gz'), parts along dimension 1, may hold values from 0 to 863, as said below
- nbr_count: int32 [16, 4, 128], P(('rep', 'gx'), 'gy', 'gz'), parts along dimension 0, may hold values from 28 to 48, as said below
- bin_counts: int32 [16, 4, 4], P('rep'), parts along dimension 0, may hold values from 2 to 32, as said below
- w_self: float32 [64, 64], replicated, may hold values from -0.75 to 0.75
- w_pair: float32 [64, 64], replicated, may hold values from -0.75 to 0.75
- w_radial: float32 [8, 64], replicated, may hold values from -2 to 2
- w_tensor: float32 [64, 64], replicated, may hold values from -0.75 to 0.75
- w_mix: float32 [128, 64], replicated, may hold values from -0.5 to 0.5
- w_out: float32 [64], replicated, may hold values from -0.75 to 0.75
Outputs:
- forces: float32 [3, 16, 4, 128], P(None, ('rep', 'gx'), 'gy', 'gz'), parts along dimension 1
- atom_energy: float32 [16, 4, 128], P(('rep', 'gx'), 'gy', 'gz'), parts along dimension 0
The draws below stay inside these ranges and needn't reach their ends.
There are 2 independent parts, one for each index of `rep`. The reference program is written for one: setup_inputs(seed, part) draws one part's arguments, and reference() takes and returns one part's arrays. A program takes and returns all parts, laid end to end along the dimension named above; an argument that names none is the same for every part. Nothing has to cross between parts.
Inputs may be any that keep to these rules, and one draw needn't show every extreme that they name: The atoms of a bin fill its slots 0 to bin_counts - 1. `nbr_index`: A code o * 32 + t names slot t of the bin at offset o = 9 (dx + 1) + 3 (dy + 1) + (dz + 1) from the atom's own bin, periodically; t is below that bin's count, and the code never names the atom itself. Neighbour slots 0 to nbr_count - 1 of an atom are valid.
All inputs are finite; a program needn't handle non-finite values.
Results may differ from the reference program's by a relative error of at most 0.0003.
Values sent between devices are 32-bit elements; how exact they have to be, the bound alone decides.
No kernel may reach another device: no remote copies, remote signals or barrier semaphores. Data moves between devices by JAX's collectives and lax.ppermute only.
A program may use at most 128 MiB of HBM per device.

```python
import jax
import jax.numpy as jnp
import numpy as np
from jax import lax

F = 64
NCH = 32
NRBF = 8
NB = 48
SLOTS = 32
NCX = 8
NCY = 4
NCZ = 4


def crowding(key):
    base_low = max(2, 3 * SLOTS // 16)
    base = jax.random.randint(jax.random.fold_in(key, 11), (NCX, NCY, NCZ), base_low, SLOTS // 2 + 1)
    dense = jax.random.randint(jax.random.fold_in(key, 12), (NCX, NCY, NCZ), 2 * SLOTS // 3, SLOTS + 1)
    anchor = jax.random.randint(jax.random.fold_in(key, 13), (), 0, NCX)
    layers = jnp.arange(NCX, dtype=jnp.int32)
    inside = (layers - anchor) % NCX < 3
    counts = jnp.where(inside[:, None, None], dense, base)
    return counts.at[anchor, 0, 0].set(SLOTS).astype(jnp.int32)


def draw_bin_counts(key, part):
    return crowding(key)


def draw_nbr_index(key, part):
    counts = crowding(key)
    key = jax.random.fold_in(key, 3)
    weights_np = []
    for code in range(27):
        reach = abs(code // 9 - 1) + abs(code // 3 % 3 - 1) + abs(code % 3 - 1)
        weights_np.append(6 if reach == 0 else 3 if reach == 1 else 1)
    lookup = jnp.asarray(np.repeat(np.arange(27), np.array(weights_np)), jnp.int32)
    shape = (NB, NCX, NCY, NCZ * SLOTS)
    picked = jax.random.randint(jax.random.fold_in(key, 1), shape, 0, lookup.shape[0])
    offset = lookup[picked]
    step_x = offset // 9 - 1
    step_y = offset // 3 % 3 - 1
    step_z = offset % 3 - 1
    cell_x = jnp.arange(NCX, dtype=jnp.int32)[None, :, None, None]
    cell_y = jnp.arange(NCY, dtype=jnp.int32)[None, None, :, None]
    flat_z = jnp.arange(NCZ * SLOTS, dtype=jnp.int32)[None, None, None, :]
    cell_z = flat_z // SLOTS
    own_slot = flat_z % SLOTS
    target = counts[(cell_x + step_x) % NCX, (cell_y + step_y) % NCY, (cell_z + step_z) % NCZ]
    raw = jax.random.randint(jax.random.fold_in(key, 2), shape, 0, 1 << 20) % target
    is_self = (offset == 13) & (raw == own_slot)
    chosen = jnp.where(is_self, (raw + 1) % target, raw)
    return (offset * SLOTS + chosen).astype(jnp.int32)


def draw_nbr_count(key, part):
    key = jax.random.fold_in(key, 5)
    counts = jax.random.randint(key, (NCX, NCY, NCZ * SLOTS), NB * 7 // 12, NB + 1)
    return counts.at[0, 0, 0].set(NB).astype(jnp.int32)


def block_levels(key, dims, split, least, high):
    level = 1.0
    for position, shards_of in split:
        draws = jax.random.uniform(jax.random.fold_in(jax.random.fold_in(key, 6), position), (shards_of,), jnp.float32, least / len(split), high / len(split))
        level = level * jnp.repeat(jnp.exp(draws), dims[position] // shards_of).reshape((-1,) + (1,) * (len(dims) - 1 - position))
    return level


def gaussian(key, extent, spread, most, cuts=(), kind=jnp.bfloat16):
    entries = jax.random.normal(key, extent, jnp.float32) * spread
    if len(cuts) > 0:
        entries = block_levels(key, extent, cuts, -0.22, 0.18) * entries
    return jnp.clip(entries, min=-most, max=most).astype(kind)


def setup_inputs(seed: int = 0, part: int = 0) -> dict:
    key_of = jax.random.split(jax.random.key(seed), 12)
    own_keys = jax.random.split(jax.random.fold_in(key_of[11], part), 12)
    positions = jnp.clip(6.0 * jax.random.uniform(own_keys[0], (3, NCX, NCY, NCZ * SLOTS), jnp.float32) ** block_levels(own_keys[0], (3, NCX, NCY, NCZ * SLOTS), ((1, 4), (2, 2), (3, 2)), -0.2, 0.2), 0.0, 6.0)
    features = gaussian(own_keys[1], (F, NCX, NCY, NCZ * SLOTS), 1.0, 6.0, ((1, 4), (2, 2), (3, 2)), jnp.float32)
    nbr_index = draw_nbr_index(jax.random.fold_in(jax.random.fold_in(key_of[11], part), 71), part)
    nbr_count = draw_nbr_count(jax.random.fold_in(jax.random.fold_in(key_of[11], part), 71), part)
    bin_counts = draw_bin_counts(jax.random.fold_in(jax.random.fold_in(key_of[11], part), 71), part)
    w_self = gaussian(key_of[5], (F, F), F ** -0.5, 0.75, (), jnp.float32)
    w_pair = gaussian(key_of[6], (F, F), F ** -0.5, 0.75, (), jnp.float32)
    w_radial = gaussian(key_of[7], (NRBF, F), NRBF ** -0.5, 2.0, (), jnp.float32)
    w_tensor = gaussian(key_of[8], (F, 2 * NCH), F ** -0.5, 0.75, (), jnp.float32)
    w_mix = gaussian(key_of[9], (F + 2 * NCH, F), (F + 2 * NCH) ** -0.5, 0.5, (), jnp.float32)
    w_out = gaussian(key_of[10], (F,), F ** -0.5, 0.75, (), jnp.float32)
    return {"positions": positions, "features": features, "nbr_index": nbr_index, "nbr_count": nbr_count, "bin_counts": bin_counts, "w_self": w_self, "w_pair": w_pair, "w_radial": w_radial, "w_tensor": w_tensor, "w_mix": w_mix, "w_out": w_out}


cell_side = 6.0
cutoff = 6.0
soften = 0.25
env_norm = 0.25
highest = lax.Precision.HIGHEST

def atom_energy(vectors, pair_terms, self_terms, edge_mask, w_radial, w_tensor, w_mix, w_out):
    squared = lax.optimization_barrier(jnp.sum(vectors * vectors, axis=0)) + soften
    distance = jnp.sqrt(squared)
    direction = vectors / distance[None]
    envelope = jnp.square(jnp.maximum(1.0 - squared / (cutoff * cutoff), 0.0)) * edge_mask
    basis_count = w_radial.shape[0]
    spacing = cutoff / (basis_count - 1)
    centres = jnp.arange(basis_count, dtype=jnp.float32) * spacing
    radial = jnp.exp(-jnp.square((distance[None] - centres[:, None, None]) / spacing))
    latent_in = self_terms[:, None, :] + pair_terms + jnp.einsum('nf,nka->fka', w_radial, radial, precision=highest)
    latent = jax.nn.silu(latent_in) * envelope[None]
    tensor_weights = jnp.einsum('fc,fka->cka', w_tensor, latent, precision=highest)
    channels = tensor_weights.shape[0] // 2
    vec_weights = tensor_weights[:channels]
    ten_weights = tensor_weights[channels:]
    identity = jnp.eye(3, dtype=jnp.float32)
    quadrupole = (direction[:, None] * direction[None, :] - identity[:, :, None, None] / 3.0).reshape((9,) + direction.shape[1:])
    vec_sums = env_norm * jnp.einsum('cka,dka->cda', vec_weights, direction, precision=highest)
    ten_sums = env_norm * jnp.einsum('cka,xka->cxa', ten_weights, quadrupole, precision=highest)
    vec_scalar = vec_weights * jnp.einsum('cda,dka->cka', vec_sums, direction, precision=highest)
    ten_scalar = ten_weights * jnp.einsum('cxa,xka->cka', ten_sums, quadrupole, precision=highest)
    feat_width = latent.shape[0]
    mixture = jnp.einsum('fg,fka->gka', w_mix[:feat_width], latent, precision=highest)
    mixture = mixture + jnp.einsum('cg,cka->gka', w_mix[feat_width:feat_width + channels], vec_scalar, precision=highest)
    mixture = mixture + jnp.einsum('cg,cka->gka', w_mix[feat_width + channels:], ten_scalar, precision=highest)
    refined = latent + jax.nn.silu(mixture) * envelope[None]
    edge_energy = jnp.einsum('f,fka->ka', w_out, refined, precision=highest)
    return lax.optimization_barrier(jnp.sum(edge_energy, axis=0))

def reference(positions, features, nbr_index, nbr_count, bin_counts, w_self, w_pair, w_radial, w_tensor, w_mix, w_out):
    plane_atoms = NCY * NCZ * SLOTS
    whole_count = NCX * plane_atoms
    flat_pos = positions.reshape(3, whole_count)
    flat_feat = features.reshape(features.shape[0], whole_count)
    pair_all = jnp.einsum('fg,fn->gn', w_pair, flat_feat, precision=highest)
    self_all = jnp.einsum('fg,fn->gn', w_self, flat_feat, precision=highest)
    slot_index = jnp.arange(NCZ * SLOTS, dtype=jnp.int32) % SLOTS
    present = (slot_index[None, None, :] < jnp.repeat(bin_counts, SLOTS, axis=2)).astype(jnp.float32)
    cell_y = jnp.arange(NCY, dtype=jnp.int32)[None, :, None]
    cell_z = (jnp.arange(NCZ * SLOTS, dtype=jnp.int32) // SLOTS)[None, None, :]
    slot_rank = jnp.arange(NB, dtype=jnp.int32)[:, None]

    def one_layer(carry, cell_x):
        gradient, energies = carry
        nbr_codes = lax.dynamic_index_in_dim(nbr_index, cell_x, 1, keepdims=False)
        offset = nbr_codes // SLOTS
        nbr_slot = nbr_codes % SLOTS
        step_x = offset // 9 - 1
        step_y = offset // 3 % 3 - 1
        step_z = offset % 3 - 1
        target = (((cell_x + step_x) % NCX * NCY + (cell_y + step_y) % NCY) * NCZ + (cell_z + step_z) % NCZ) * SLOTS + nbr_slot
        flat_target = target.reshape(-1)
        own_index = cell_x * plane_atoms + jnp.arange(plane_atoms, dtype=jnp.int32)
        image_shift = cell_side * jnp.stack([step_x, step_y, step_z]).reshape(3, NB, plane_atoms).astype(jnp.float32)
        vectors = jnp.take(flat_pos, flat_target, axis=1).reshape(3, NB, plane_atoms) - jnp.take(flat_pos, own_index, axis=1)[:, None, :] + image_shift
        pair_terms = jnp.take(pair_all, flat_target, axis=1).reshape(-1, NB, plane_atoms)
        self_terms = jnp.take(self_all, own_index, axis=1)
        limits = lax.dynamic_index_in_dim(nbr_count, cell_x, 0, keepdims=False).reshape(plane_atoms)
        present_row = lax.dynamic_index_in_dim(present, cell_x, 0, keepdims=False).reshape(plane_atoms)
        edge_mask = (slot_rank < limits[None, :]).astype(jnp.float32) * present_row[None, :]

        def energy_of(moved):
            return atom_energy(moved, pair_terms, self_terms, edge_mask, w_radial, w_tensor, w_mix, w_out)
        atom_values, backward = jax.vjp(energy_of, vectors)
        pulled, = backward(jnp.ones_like(atom_values))
        gradient = gradient.at[:, flat_target].add(pulled.reshape(3, -1))
        gradient = gradient.at[:, own_index].add(-lax.optimization_barrier(jnp.sum(pulled, axis=1)))
        energies = energies.at[own_index].add(atom_values)
        return ((gradient, energies), None)
    initial = (jnp.zeros((3, whole_count), jnp.float32), jnp.zeros((whole_count,), jnp.float32))
    (gradient, energies), unused = lax.scan(one_layer, initial, jnp.arange(NCX, dtype=jnp.int32))
    forces = -gradient.reshape(3, NCX, NCY, NCZ * SLOTS)
    return (forces, energies.reshape(NCX, NCY, NCZ * SLOTS))
```

```python
import functools

import jax
import jax.numpy as jnp
from jax import lax
from jax.experimental import pallas as pl
from jax.experimental.pallas import tpu as pltpu
from jax.sharding import PartitionSpec as P

SLOTS = 32
cell_side = 6.0
cutoff = 6.0
soften = 0.25
env_norm = 0.25
root2 = 2.0**0.5
f32 = jnp.float32
bf16 = jnp.bfloat16
HALF = 24
WIDE = 256
FEAT = 64
ROWS = 72

U, Q, ENV, DIST, INV, VEC, DENV, GEO = 0, 3, 9, 10, 11, 12, 15, 16


def halves(x):
    hi = x.astype(bf16)
    return hi, (x - hi.astype(f32)).astype(bf16)


def stacked(x):
    hi, lo = halves(x)
    return jnp.concatenate([hi, lo, hi], axis=0)


def stacked_left(w):
    hi, lo = halves(w)
    return jnp.concatenate([hi, hi, lo], axis=1)


def dot(a, b):
    return jnp.dot(a, b, preferred_element_type=f32)


def small_stack(x):
    hi, lo = halves(x)
    hi, lo = hi.astype(f32), lo.astype(f32)
    return jnp.concatenate([hi, lo, hi, jnp.zeros_like(hi)], axis=0)


def sigmoid(x):
    return 0.5 + 0.5 * jnp.tanh(0.5 * x)


def prepare(
    w_self, w_pair, w_radial, w_tensor, w_mix, w_out, p_a, p_b, p_c, p_d, p_r, p_e, p_p, p_s, p_col
):
    tensor, mix, out_row = w_tensor[...], w_mix[...], w_out[...]
    first = jnp.concatenate(
        [tensor.T, mix[:FEAT].T, jnp.broadcast_to(out_row, (8, FEAT))], axis=0
    )
    p_a[...] = stacked_left(first)
    p_b[...] = stacked_left(mix[FEAT:].T)
    p_c[...] = stacked_left(mix * out_row)
    p_d[...] = stacked_left(tensor)
    radial = w_radial[...]
    hi, lo = halves(radial)
    hi, lo = hi.astype(f32), lo.astype(f32)
    p_r[...] = jnp.concatenate([hi, hi, lo, jnp.zeros_like(hi)], axis=0).T.astype(bf16)
    p_e[...] = stacked_left(jnp.concatenate([radial, jnp.zeros_like(radial)], axis=0))
    p_p[...] = stacked_left(w_pair[...].T)
    p_s[...] = stacked_left(w_self[...].T)
    p_col[...] = jnp.broadcast_to(out_row, (128, FEAT)).T


def layer(
    which,
    ghost,
    core,
    codes,
    limit,
    w_a,
    w_b,
    w_c,
    w_d,
    w_r,
    w_e,
    w_p,
    w_s,
    w_col,
    out,
    energy,
    pair,
    self_t,
    lane_i,
    col_i,
    geo,
    act,
    slope,
    tens,
    mix0,
    prod,
    back,
    resid,
    e_row,
    m_row,
    d_row,
    du_row,
    dr_row,
    v_acc,
    dv_acc,
    g_row,
    s_acc,
    own_sum,
):
    def source(dx, yc):
        if which == 0:
            return ghost.at[yc] if dx == 0 else core.at[dx - 1, yc]
        return ghost.at[yc] if dx == 2 else core.at[dx, yc]

    lanes = lax.broadcasted_iota(jnp.int32, (1, 128), 1)

    def both(x):
        return jnp.where(lanes < 64, pltpu.roll(x, 96, 1), pltpu.roll(x, 32, 1))

    for dx in range(3):
        rows = jnp.concatenate([source(dx, yc)[:FEAT, :] for yc in range(4)], axis=1)
        terms = dot(w_p[...], stacked(rows))
        for yc in range(4):
            pair[dx * 4 + yc] = terms[:, 128 * yc : 128 * yc + 128]
    rows = jnp.concatenate([source(1, 1 + y)[:FEAT, :] for y in range(2)], axis=1)
    terms = dot(w_s[...], stacked(rows))
    for y in range(2):
        self_t[:, 128 * y : 128 * y + 128] = both(terms[:, 128 * y : 128 * y + 128])

    code = codes[...]
    offset = code >> 5
    column = (offset * 43) >> 7
    dz = offset - 3 * column
    dx = (offset * 57) >> 9
    dy = column - 3 * dx
    lane256 = lax.broadcasted_iota(jnp.int32, (HALF, WIDE), 1)
    z_own = (lane256 >> 5) & 1
    lane_i[...] = ((z_own + dz) << 5) + (code & 31)
    col_i[...] = column
    rank = lax.broadcasted_iota(jnp.int32, (HALF, WIDE), 0) + HALF * ((lane256 >> 6) & 1)
    mask = (rank < limit[...]).astype(f32)

    steps = (dx, dy, dz)
    vec = []
    for d in range(3):
        found = []
        for y in range(2):
            own = both(source(1, 1 + y)[FEAT + d : FEAT + d + 1, :])
            parts = []
            for j in range(HALF // 8):
                where = (slice(8 * j, 8 * j + 8), slice(128 * y, 128 * y + 128))
                lane, col = lane_i[where], col_i[where]
                acc = None
                for c in range(9):
                    row = source(c // 3, y + c % 3)[FEAT + d : FEAT + d + 1, :]
                    value = jnp.take_along_axis(
                        jnp.broadcast_to(row, (8, 128)), lane, axis=1, mode="promise_in_bounds"
                    )
                    acc = value if c == 0 else jnp.where(col == c, value, acc)
                parts.append(acc)
            found.append(jnp.concatenate(parts, axis=0) - own)
        vec.append(
            jnp.concatenate(found, axis=1) + cell_side * (steps[d] - 1).astype(f32)
        )
    squared = vec[0] * vec[0] + vec[1] * vec[1] + vec[2] * vec[2] + soften
    dist = jnp.sqrt(squared)
    inv = 1.0 / dist
    u = [v * inv for v in vec]
    taper = jnp.maximum(1.0 - squared / (cutoff * cutoff), 0.0)
    for d in range(3):
        geo[U + d] = u[d]
        geo[VEC + d] = vec[d]
        geo[Q + d] = u[d] * u[d] - 1.0 / 3.0
    geo[Q + 3] = root2 * u[0] * u[1]
    geo[Q + 4] = root2 * u[0] * u[2]
    geo[Q + 5] = root2 * u[1] * u[2]
    geo[ENV] = taper * taper * mask
    geo[DENV] = taper * mask * (-2.0 / (cutoff * cutoff))
    geo[DIST] = dist
    geo[INV] = inv

    spacing = cutoff / (w_e.shape[0] // 2 - 1)
    level = lax.broadcasted_iota(jnp.int32, (8, 1), 0).astype(f32)

    def row(k, s):
        return geo[k, pl.ds(s, 1), :]

    def basis(s):
        x = row(DIST, s) / spacing - level
        return x, jnp.exp(-x * x)

    v_acc[...] = jnp.zeros_like(v_acc)
    dv_acc[...] = jnp.zeros_like(dv_acc)

    @pl.loop(0, HALF, unroll=2)
    def forward(s):
        lane_s = lane_i[pl.ds(s, 1), :]
        col_s = col_i[pl.ds(s, 1), :]
        sides = []
        for y in range(2):
            lane = jnp.broadcast_to(lane_s[:, 128 * y : 128 * y + 128], (8, 128))
            col = jnp.broadcast_to(col_s[:, 128 * y : 128 * y + 128], (8, 128))
            masks = [col == c for c in range(9)]
            groups = []
            for g in range(FEAT // 8):
                acc = None
                for c in range(9):
                    value = jnp.take_along_axis(
                        pair[(c // 3) * 4 + y + c % 3, 8 * g : 8 * g + 8, :],
                        lane,
                        axis=1,
                        mode="promise_in_bounds",
                    )
                    acc = value if c == 0 else jnp.where(masks[c], value, acc)
                groups.append(acc)
            sides.append(jnp.concatenate(groups, axis=0))
        terms = jnp.concatenate(sides, axis=1)
        _, waves = basis(s)
        z = dot(w_r[...], small_stack(waves).astype(bf16)) + (self_t[...] + terms)
        sg = sigmoid(z)
        silu = z * sg
        env = row(ENV, s)
        act[s] = silu
        slope[s] = (sg + silu * (1.0 - sg)) * env
        both_t = dot(w_a[...], stacked(silu * env))
        tens[s] = both_t[:FEAT]
        mix0[s] = both_t[FEAT : 2 * FEAT]
        e_row[pl.ds(s, 1), :] = both_t[2 * FEAT : 2 * FEAT + 1]
        for k in range(9):
            part = both_t[:32] if k < 3 else both_t[32:64]
            v_acc[k] += part * row(k, s)

    def folded(x):
        return jnp.concatenate(
            [
                env_norm * (x[:, c : c + 128] + pltpu.roll(x[:, c : c + 128], 64, 1))
                for c in (0, 128)
            ],
            axis=1,
        )

    for k in range(9):
        v_acc[k] = folded(v_acc[k])
    col_w = jnp.concatenate([w_col[...], w_col[...]], axis=1)

    @pl.loop(0, HALF, unroll=2)
    def middle(s):
        t = tens[s]
        vec_in = v_acc[0] * row(0, s)
        for k in range(1, 3):
            vec_in += v_acc[k] * row(k, s)
        ten_in = v_acc[3] * row(3, s)
        for k in range(4, 9):
            ten_in += v_acc[k] * row(k, s)
        inner = jnp.concatenate([vec_in, ten_in], axis=0)
        mixture = mix0[s] + dot(w_b[...], stacked(t * inner))
        sg = sigmoid(mixture)
        silu = mixture * sg
        m_row[pl.ds(s, 1), :] = jnp.sum(col_w * silu, axis=0, keepdims=True)
        grad = (sg + silu * (1.0 - sg)) * row(ENV, s)
        pulled = dot(w_c[...], stacked(grad))
        resid[s] = pulled[:FEAT] + col_w
        dvt = pulled[FEAT:]
        back[s] = dvt * inner
        p = dvt * t
        prod[s] = p
        for k in range(9):
            part = p[:32] if k < 3 else p[32:]
            dv_acc[k] += part * row(k, s)

    for k in range(9):
        dv_acc[k] = folded(dv_acc[k])

    @pl.loop(0, HALF, unroll=2)
    def backward(s):
        t = tens[s]
        p = prod[s]
        dt = back[s]
        vec_part, ten_part = dt[:32], dt[32:]
        for k in range(9):
            half = slice(0, 32) if k < 3 else slice(32, 64)
            moved = dv_acc[k]
            if k < 3:
                vec_part += moved * row(k, s)
            else:
                ten_part += moved * row(k, s)
            du_row[k, pl.ds(s, 1), :] = jnp.sum(
                p[half] * v_acc[k] + t[half] * moved, axis=0, keepdims=True
            )
        dl = resid[s] + dot(w_d[...], stacked(jnp.concatenate([vec_part, ten_part], axis=0)))
        d_row[pl.ds(s, 1), :] = jnp.sum(dl * act[s], axis=0, keepdims=True)
        dwaves = dot(w_e[...], stacked(dl * slope[s]))[:8]
        x, waves = basis(s)
        dr_row[pl.ds(s, 1), :] = jnp.sum(dwaves * waves * x, axis=0, keepdims=True)

    env, m_sum = geo[ENV], m_row[...]
    values = jnp.sum(e_row[...] + env * m_sum, axis=0, keepdims=True)
    energy[...] = jnp.broadcast_to(fold_sides(values), energy.shape)
    u = [geo[U + d] for d in range(3)]
    du = [du_row[d] for d in range(3)]
    dq = [du_row[3 + k] for k in range(6)]
    cross = ((0, 1, 3), (0, 2, 4), (1, 2, 5))
    du = [du[d] + 2.0 * u[d] * dq[d] for d in range(3)]
    for a, b, k in cross:
        du[a] = du[a] + root2 * u[b] * dq[k]
        du[b] = du[b] + root2 * u[a] * dq[k]
    inv = geo[INV]
    along = du[0] * u[0] + du[1] * u[1] + du[2] * u[2]
    dr = dr_row[...] * (-2.0 / spacing) - along * inv
    ds = 2.0 * geo[DENV] * (d_row[...] + m_sum) + dr * inv
    zero = jnp.zeros((HALF, WIDE), f32)
    for d in range(3):
        g = du[d] * inv + geo[VEC + d] * ds
        hi, lo = halves(g)
        g_row[:, d, :] = hi.astype(f32)
        g_row[:, 3 + d, :] = lo.astype(f32)
        own = fold_sides(jnp.sum(g, axis=0, keepdims=True))
        own_sum[d : d + 1, :] = own
    g_row[:, 6, :] = zero
    g_row[:, 7, :] = zero

    s_acc[...] = jnp.zeros_like(s_acc)
    places = lax.broadcasted_iota(jnp.int32, (128, 128), 0)

    @pl.loop(0, HALF // 4)
    def scatter(q):
        for y in range(2):
            side = slice(128 * y, 128 * y + 128)
            left, right = [], []
            for i in range(4):
                s = 4 * q + i
                lane = lane_i[pl.ds(s, 1), :][:, side]
                col = jnp.broadcast_to(col_i[pl.ds(s, 1), :][:, side], (8, 128))
                tile = g_row[s, :, side]
                left.append(
                    jnp.concatenate(
                        [jnp.where(col == c, tile, 0.0) for c in range(9)], axis=0
                    ).astype(bf16)
                )
                right.append((places == lane).astype(f32).astype(bf16))
            s_acc[y] += lax.dot_general(
                jnp.concatenate(left, axis=1),
                jnp.concatenate(right, axis=1),
                (((1,), (1,)), ((), ())),
                preferred_element_type=f32,
            )

    out[...] = jnp.zeros_like(out)
    for y in range(2):
        for c in range(9):
            tile = s_acc[y, 8 * c : 8 * c + 8, :]
            out[c // 3, y + c % 3, 0:3, :] += tile[0:3] + tile[3:6]
        own = pltpu.roll(own_sum[:, 128 * y : 128 * y + 128], 32, 1)
        kept = jnp.where((lanes >= 32) & (lanes < 96), own, 0.0)
        out[1, 1 + y, 0:3, :] -= kept[0:3]


def fold_sides(x):
    return jnp.concatenate(
        [x[:, c : c + 128] + pltpu.roll(x[:, c : c + 128], 64, 1) for c in (0, 128)], axis=1
    )


def run_prepare(*weights):
    shapes = ((136, 192), (64, 192), (128, 192), (64, 192), (64, 32), (16, 192), (64, 192), (64, 192))
    outs = [jax.ShapeDtypeStruct(shape, bf16) for shape in shapes]
    outs.append(jax.ShapeDtypeStruct((FEAT, 128), f32))
    return pl.pallas_call(prepare, out_shape=outs)(*weights)


def run_layer(which, ghost, core, codes, limit, weights):
    big = pltpu.VMEM((HALF, FEAT, WIDE), f32)
    flat = pltpu.VMEM((HALF, WIDE), f32)
    index = pltpu.VMEM((HALF, WIDE), jnp.int32)
    sums = pltpu.VMEM((9, 32, WIDE), f32)
    scratch = [
        pltpu.VMEM((12, FEAT, 128), f32),
        pltpu.VMEM((FEAT, WIDE), f32),
        index,
        index,
        pltpu.VMEM((GEO, HALF, WIDE), f32),
        big,
        big,
        big,
        big,
        big,
        big,
        big,
        flat,
        flat,
        flat,
        pltpu.VMEM((9, HALF, WIDE), f32),
        flat,
        sums,
        sums,
        pltpu.VMEM((HALF, 8, WIDE), f32),
        pltpu.VMEM((2, 72, 128), f32),
        pltpu.VMEM((8, WIDE), f32),
    ]
    return pl.pallas_call(
        functools.partial(layer, which),
        out_shape=[
            jax.ShapeDtypeStruct((3, 4, 8, 128), f32),
            jax.ShapeDtypeStruct((8, WIDE), f32),
        ],
        scratch_shapes=scratch,
        compiler_params=pltpu.CompilerParams(vmem_limit_bytes=40 * 2**20),
    )(ghost, core, codes, limit, *weights)


def shifts(axis):
    size = lax.axis_size(axis)
    up = [(i, (i + 1) % size) for i in range(size)]
    return up, [(j, i) for i, j in up]


def exchange(low, high, axis, joined):
    up, down = shifts(axis)
    if lax.axis_size(axis) == 2:
        got = lax.ppermute(joined((high, low)), axis, up)
        size = got.shape[-1] // 2 if joined is last_joined else got.shape[1] // 2
        if joined is last_joined:
            return got[..., :size], got[..., size:]
        return got[:, :size], got[:, size:]
    return lax.ppermute(high, axis, up), lax.ppermute(low, axis, down)


def last_joined(parts):
    return jnp.concatenate(parts, axis=-1)


def second_joined(parts):
    return jnp.concatenate(parts, axis=1)


def local(
    positions,
    features,
    nbr_index,
    nbr_count,
    bin_counts,
    w_self,
    w_pair,
    w_radial,
    w_tensor,
    w_mix,
    w_out,
):
    cells_x, cells_y = nbr_count.shape[:2]
    cells_z = nbr_count.shape[2] // SLOTS
    lanes = cells_z * SLOTS
    weights = run_prepare(w_self, w_pair, w_radial, w_tensor, w_mix, w_out[None])

    x_index = lax.axis_index("gx")
    y_index = lax.axis_index("gy")
    z_index = lax.axis_index("gz")
    own_counts = lax.dynamic_slice(
        bin_counts,
        (x_index * cells_x, y_index * cells_y, z_index * cells_z),
        (cells_x, cells_y, cells_z),
    )
    slot = jnp.arange(lanes, dtype=jnp.int32) % SLOTS
    limit = jnp.where(slot < jnp.repeat(own_counts, SLOTS, axis=2), nbr_count, 0)
    limit = jnp.broadcast_to(limit[:, :, None, :], (cells_x, cells_y, 2, lanes))
    limit = limit.reshape(cells_x, 1, WIDE)
    codes = nbr_index.reshape(2, HALF, cells_x, cells_y, lanes)
    codes = codes.transpose(2, 1, 3, 0, 4).reshape(cells_x, HALF, WIDE)

    fill = jnp.zeros((ROWS - FEAT - 3,) + positions.shape[1:], f32)
    state = jnp.concatenate([features, positions, fill], axis=0).transpose(1, 2, 0, 3)
    below, above = exchange(state[..., :SLOTS], state[..., -SLOTS:], "gz", last_joined)
    state = jnp.concatenate([below, state, above], axis=-1)
    below, above = exchange(state[:, :1], state[:, -1:], "gy", second_joined)
    core = jnp.concatenate([below, state, above], axis=1)
    up, down = shifts("gx")
    under = lax.ppermute(core[-1], "gx", up)
    over = lax.ppermute(core[0], "gx", down)

    grad0, energy0 = run_layer(0, under, core, codes[0], limit[0], weights)
    back0 = lax.ppermute(grad0[0, :, :4], "gx", down)
    grad1, energy1 = run_layer(1, over, core, codes[1], limit[1], weights)
    back1 = lax.ppermute(grad1[2, :, :4], "gx", up)

    grad = jnp.stack(
        [grad0[1, :, :4] + grad1[0, :, :4] + back1, grad0[2, :, :4] + grad1[1, :, :4] + back0]
    )
    below, above = exchange(grad[:, :1], grad[:, -1:], "gy", second_joined)
    grad = grad[:, 1:-1] + jnp.concatenate([below, above], axis=1)
    below, above = exchange(grad[..., :SLOTS], grad[..., -SLOTS:], "gz", last_joined)
    grad = grad[..., SLOTS:-SLOTS] + jnp.concatenate([below, above], axis=-1)
    forces = -grad[:, :, :3].transpose(2, 0, 1, 3)
    energies = jnp.stack([energy0[0], energy1[0]]).reshape(cells_x, cells_y, 2, lanes)[:, :, 0]
    return forces, energies


def solution(mesh):
    return jax.shard_map(
        local,
        mesh=mesh,
        in_specs=(
            P(None, ("rep", "gx"), "gy", "gz"),
            P(None, ("rep", "gx"), "gy", "gz"),
            P(None, ("rep", "gx"), "gy", "gz"),
            P(("rep", "gx"), "gy", "gz"),
            P("rep", None, None),
            P(),
            P(),
            P(),
            P(),
            P(),
            P(),
        ),
        out_specs=(P(None, ("rep", "gx"), "gy", "gz"), P(("rep", "gx"), "gy", "gz")),
        check_vma=False,
    )
```

```python
import functools

import jax
import jax.numpy as jnp
from jax import lax
from jax.experimental import pallas as pl
from jax.experimental.pallas import tpu as pltpu
from jax.sharding import PartitionSpec as P

SLOTS = 32
cell_side = 6.0
cutoff = 6.0
soften = 0.25
env_norm = 0.25
root2 = 2.0**0.5
f32 = jnp.float32
bf16 = jnp.bfloat16
HALF = 24
WIDE = 256
FEAT = 64
ROWS = 72
BASIS = 8
MIRRORED = 64
SPACING = cutoff / (BASIS - 1)
GROUP = 4
UNROLL = 1

U, Q, ENV, DIST, INV, VEC, DENV, GEO = 0, 3, 9, 10, 11, 12, 15, 16


def halves(x):
    hi = x.astype(bf16)
    return hi, (x - hi.astype(f32)).astype(bf16)


def stacked(x):
    hi, lo = halves(x)
    return jnp.concatenate([hi, lo, hi], axis=0)


def stacked_left(w):
    hi, lo = halves(w)
    return jnp.concatenate([hi, hi, lo], axis=1)


def dot(a, b):
    return jnp.dot(a, b, preferred_element_type=f32)


def small_stack(x):
    hi, lo = halves(x)
    hi, lo = hi.astype(f32), lo.astype(f32)
    return jnp.concatenate([hi, lo, hi, jnp.zeros_like(hi)], axis=0)


def sigmoid(x):
    return 0.5 + 0.5 * jnp.tanh(0.5 * x)


W_A, W_B, W_C, W_D, W_E, W_P, W_S, W_R, W_END = 0, 144, 208, 336, 400, 416, 480, 544, 608


def pipeline(stages, last=None):
    groups, depth = HALF // GROUP, len(stages)

    def step(t, first, stop):
        for k in range(stop - 1, first - 1, -1):
            start = (t - k) * GROUP
            for i in range(GROUP):
                stages[k](start + i, i)
            if k == depth - 1 and last is not None:
                last(start)

    for t in range(depth - 1):
        step(t, 0, t + 1)
    pl.loop(depth - 1, groups, unroll=UNROLL)(lambda t: step(t, 0, depth))
    for t in range(groups, groups + depth - 1):
        step(t, t - groups + 1, depth)


def basis(dist):
    level = lax.broadcasted_iota(jnp.int32, (BASIS, 1), 0).astype(f32)
    x = dist / SPACING - level
    return x, jnp.exp(-x * x)


def lane_row():
    return lax.broadcasted_iota(jnp.int32, (1, 128), 1)


def fold_sides(x):
    return jnp.concatenate(
        [x[:, c : c + 128] + pltpu.roll(x[:, c : c + 128], 64, 1) for c in (0, 128)], axis=1
    )


def prepare(w_self, w_pair, w_radial, w_tensor, mix_t, w_out, merged):
    tensor, mix, out_row = w_tensor[...], mix_t[...].T, w_out[...]
    parts = (
        jnp.concatenate(
            [tensor.T, mix_t[:, :FEAT], jnp.broadcast_to(out_row, (16, FEAT))], axis=0
        ),
        mix_t[:, FEAT:],
        mix * out_row,
        tensor,
        jnp.concatenate([w_radial[...], jnp.zeros_like(w_radial)], axis=0),
        w_pair[...].T,
        w_self[...].T,
    )
    for first, part in zip((W_A, W_B, W_C, W_D, W_E, W_P, W_S), parts):
        merged[first : first + part.shape[0], :] = stacked_left(part)
    hi, lo = halves(w_radial[...])
    hi, lo = hi.astype(f32), lo.astype(f32)
    rows = jnp.concatenate([hi, hi, lo, jnp.zeros((168, FEAT), f32)], axis=0)
    merged[W_R:W_END, :] = rows.T.astype(bf16)


def front(
    which,
    ghost_own,
    ghost_sides,
    core_own,
    core_sides,
    codes,
    limit,
    merged,
    act,
    slope,
    tens,
    mix0,
    v_acc,
    e_row,
    geo,
    lane_i,
    col_i,
    pair,
    self_t,
    step_a,
    step_b,
):
    w_a = merged.at[W_A:W_B]
    w_p, w_s = merged.at[W_P:W_S], merged.at[W_S:W_R]
    w_r = merged.at[W_R:W_END, 0 : 4 * BASIS]

    def source(dx, yc):
        here = yc - 1 if yc in (1, 2) else yc // 3
        own, sides = (ghost_own, ghost_sides), (core_own, core_sides)
        if dx == (0 if which == 0 else 2):
            return own[yc in (0, 3)].at[here]
        return sides[yc in (0, 3)].at[dx - 1 + which, here]

    lanes = lane_row()

    def both(x):
        return jnp.where(lanes < 64, pltpu.roll(x, 96, 1), pltpu.roll(x, 32, 1))

    for dx in range(3):
        rows = jnp.concatenate([source(dx, yc)[:FEAT, :] for yc in range(4)], axis=1)
        terms = dot(w_p[...], stacked(rows))
        for yc in range(4):
            pair[dx * 4 + yc] = terms[:, 128 * yc : 128 * yc + 128]
    rows = jnp.concatenate([source(1, 1 + y)[:FEAT, :] for y in range(2)], axis=1)
    terms = dot(w_s[...], stacked(rows))
    for y in range(2):
        self_t[:, 128 * y : 128 * y + 128] = both(terms[:, 128 * y : 128 * y + 128])

    code = codes[...]
    offset = code >> 5
    plane = (offset * 43) >> 7
    dz = offset - 3 * plane
    dx = (offset * 57) >> 9
    dy = plane - 3 * dx
    limits = limit[...]
    mirrored = jnp.where(limits >= MIRRORED, 2 - dx, dx)
    lane256 = lax.broadcasted_iota(jnp.int32, (HALF, WIDE), 1)
    z_own = (lane256 >> 5) & 1
    lane_i[...] = ((z_own + dz) << 5) + (code & 31)
    col_i[...] = 3 * mirrored + dy
    rank = lax.broadcasted_iota(jnp.int32, (HALF, WIDE), 0) + HALF * ((lane256 >> 6) & 1)
    mask = (rank < (limits & (MIRRORED - 1))).astype(f32)

    steps = (dx, dy, dz)
    vec = []
    for d in range(3):
        found = []
        for y in range(2):
            own = both(source(1, 1 + y)[FEAT + d : FEAT + d + 1, :])
            parts = []
            for j in range(HALF // 8):
                where = (slice(8 * j, 8 * j + 8), slice(128 * y, 128 * y + 128))
                lane, col = lane_i[where], col_i[where]
                acc = None
                for c in range(9):
                    row = source(c // 3, y + c % 3)[FEAT + d : FEAT + d + 1, :]
                    value = jnp.take_along_axis(
                        jnp.broadcast_to(row, (8, 128)), lane, axis=1, mode="promise_in_bounds"
                    )
                    acc = value if c == 0 else jnp.where(col == c, value, acc)
                parts.append(acc)
            found.append(jnp.concatenate(parts, axis=0) - own)
        vec.append(
            jnp.concatenate(found, axis=1) + cell_side * (steps[d] - 1).astype(f32)
        )
    squared = vec[0] * vec[0] + vec[1] * vec[1] + vec[2] * vec[2] + soften
    dist = jnp.sqrt(squared)
    inv = 1.0 / dist
    u = [v * inv for v in vec]
    taper = jnp.maximum(1.0 - squared / (cutoff * cutoff), 0.0)
    for d in range(3):
        geo[U + d] = u[d]
        geo[VEC + d] = vec[d]
        geo[Q + d] = u[d] * u[d] - 1.0 / 3.0
    geo[Q + 3] = root2 * u[0] * u[1]
    geo[Q + 4] = root2 * u[0] * u[2]
    geo[Q + 5] = root2 * u[1] * u[2]
    geo[ENV] = taper * taper * mask
    geo[DENV] = taper * mask * (-2.0 / (cutoff * cutoff))
    geo[DIST] = dist
    geo[INV] = inv

    def row(k, s):
        return geo[k, pl.ds(s, 1), :]

    v_acc[...] = jnp.zeros_like(v_acc)

    def gathered(s):
        lane_s = lane_i[pl.ds(s, 1), :]
        col_s = col_i[pl.ds(s, 1), :]
        sides = []
        for y in range(2):
            lane = jnp.broadcast_to(lane_s[:, 128 * y : 128 * y + 128], (8, 128))
            col = jnp.broadcast_to(col_s[:, 128 * y : 128 * y + 128], (8, 128))
            masks = [col == c for c in range(9)]
            groups = []
            for g in range(FEAT // 8):
                acc = None
                for c in range(9):
                    value = jnp.take_along_axis(
                        pair[(c // 3) * 4 + y + c % 3, 8 * g : 8 * g + 8, :],
                        lane,
                        axis=1,
                        mode="promise_in_bounds",
                    )
                    acc = value if c == 0 else jnp.where(masks[c], value, acc)
                groups.append(acc)
            sides.append(jnp.concatenate(groups, axis=0))
        return jnp.concatenate(sides, axis=1)

    def forward_a(s, i):
        _, waves = basis(row(DIST, s))
        step_a[i] = dot(w_r[...], small_stack(waves).astype(bf16)) + (self_t[...] + gathered(s))

    def forward_b(s, i):
        z = step_a[i]
        sg = sigmoid(z)
        silu = z * sg
        env = row(ENV, s)
        act[s] = silu
        slope[s] = (sg + silu * (1.0 - sg)) * env
        step_b[i] = dot(w_a[...], stacked(silu * env))

    def forward_c(s, i):
        both_t = step_b[i]
        tens[s] = both_t[:FEAT]
        mix0[s] = both_t[FEAT : 2 * FEAT]
        e_row[pl.ds(s, 1), :] = both_t[2 * FEAT : 2 * FEAT + 1]

    def forward_sum(first):
        for k in range(9):
            part = slice(0, 32) if k < 3 else slice(32, 64)
            total = v_acc[k]
            for i in range(GROUP):
                total += step_b[i, part] * row(k, first + i)
            v_acc[k] = total

    pipeline((forward_a, forward_b, forward_c), forward_sum)

    for k in range(9):
        v_acc[k] = env_norm * fold_sides(v_acc[k])


def rear(
    merged,
    out_row,
    added,
    act,
    slope,
    tens,
    mix0,
    v_acc,
    e_row,
    geo,
    lane_i,
    col_i,
    out,
    energy,
    step_a,
    step_b,
    step_c,
    prod,
    back,
    resid,
    m_row,
    d_row,
    du_row,
    dr_row,
    dv_acc,
    g_row,
    s_acc,
    own_sum,
):
    w_b, w_c = merged.at[W_B:W_C], merged.at[W_C:W_D]
    w_d, w_e = merged.at[W_D:W_E], merged.at[W_E:W_P]
    lanes = lane_row()

    def row(k, s):
        return geo[k, pl.ds(s, 1), :]

    dv_acc[...] = jnp.zeros_like(dv_acc)
    col_w = jnp.broadcast_to(out_row[...], (128, FEAT)).T
    col_w = jnp.concatenate([col_w, col_w], axis=1)

    def middle_a(s, i):
        vec_in = v_acc[0] * row(0, s)
        for k in range(1, 3):
            vec_in += v_acc[k] * row(k, s)
        ten_in = v_acc[3] * row(3, s)
        for k in range(4, 9):
            ten_in += v_acc[k] * row(k, s)
        inner = jnp.concatenate([vec_in, ten_in], axis=0)
        back[s] = inner
        step_a[i] = mix0[s] + dot(w_b[...], stacked(tens[s] * inner))

    def middle_b(s, i):
        mixture = step_a[i]
        sg = sigmoid(mixture)
        silu = mixture * sg
        m_row[pl.ds(s, 1), :] = jnp.sum(col_w * silu, axis=0, keepdims=True)
        grad = (sg + silu * (1.0 - sg)) * row(ENV, s)
        step_b[i, : 2 * FEAT] = dot(w_c[...], stacked(grad))

    def middle_c(s, i):
        resid[s] = step_b[i, :FEAT] + col_w
        dvt = step_b[i, FEAT : 2 * FEAT]
        back[s] = dvt * back[s]
        p = dvt * tens[s]
        prod[s] = p
        step_c[i] = p

    def middle_sum(first):
        for k in range(9):
            part = slice(0, 32) if k < 3 else slice(32, 64)
            total = dv_acc[k]
            for i in range(GROUP):
                total += step_c[i, part] * row(k, first + i)
            dv_acc[k] = total

    pipeline((middle_a, middle_b, middle_c), middle_sum)

    for k in range(9):
        dv_acc[k] = env_norm * fold_sides(dv_acc[k])

    def backward_a(s, i):
        t = tens[s]
        p = prod[s]
        dt = back[s]
        vec_part, ten_part = dt[:32], dt[32:]
        for k in range(9):
            half = slice(0, 32) if k < 3 else slice(32, 64)
            moved = dv_acc[k]
            if k < 3:
                vec_part += moved * row(k, s)
            else:
                ten_part += moved * row(k, s)
            du_row[k, pl.ds(s, 1), :] = jnp.sum(
                p[half] * v_acc[k] + t[half] * moved, axis=0, keepdims=True
            )
        step_a[i] = resid[s] + dot(
            w_d[...], stacked(jnp.concatenate([vec_part, ten_part], axis=0))
        )

    def backward_b(s, i):
        dl = step_a[i]
        d_row[pl.ds(s, 1), :] = jnp.sum(dl * act[s], axis=0, keepdims=True)
        step_b[i, :16] = dot(w_e[...], stacked(dl * slope[s]))

    def backward_c(s, i):
        x, waves = basis(row(DIST, s))
        dr_row[pl.ds(s, 1), :] = jnp.sum(step_b[i, :8] * waves * x, axis=0, keepdims=True)

    pipeline((backward_a, backward_b, backward_c))

    env, m_sum = geo[ENV], m_row[...]
    values = jnp.sum(e_row[...] + env * m_sum, axis=0, keepdims=True)
    energy[...] = jnp.broadcast_to(fold_sides(values), energy.shape)
    u = [geo[U + d] for d in range(3)]
    du = [du_row[d] for d in range(3)]
    dq = [du_row[3 + k] for k in range(6)]
    cross = ((0, 1, 3), (0, 2, 4), (1, 2, 5))
    du = [du[d] + 2.0 * u[d] * dq[d] for d in range(3)]
    for a, b, k in cross:
        du[a] = du[a] + root2 * u[b] * dq[k]
        du[b] = du[b] + root2 * u[a] * dq[k]
    inv = geo[INV]
    along = du[0] * u[0] + du[1] * u[1] + du[2] * u[2]
    dr = dr_row[...] * (-2.0 / SPACING) - along * inv
    ds = 2.0 * geo[DENV] * (d_row[...] + m_sum) + dr * inv
    zero = jnp.zeros((HALF, WIDE), f32)
    for d in range(3):
        g = du[d] * inv + geo[VEC + d] * ds
        hi, lo = halves(g)
        g_row[:, d, :] = hi.astype(f32)
        g_row[:, 3 + d, :] = lo.astype(f32)
        own = fold_sides(jnp.sum(g, axis=0, keepdims=True))
        own_sum[d : d + 1, :] = own
    g_row[:, 6, :] = zero
    g_row[:, 7, :] = zero

    s_acc[...] = jnp.zeros_like(s_acc)
    places = lax.broadcasted_iota(jnp.int32, (128, 128), 0)

    @pl.loop(0, HALF // 4, unroll=3)
    def scatter(q):
        for y in range(2):
            side = slice(128 * y, 128 * y + 128)
            left, right = [], []
            for i in range(4):
                s = 4 * q + i
                lane = lane_i[pl.ds(s, 1), :][:, side]
                col = jnp.broadcast_to(col_i[pl.ds(s, 1), :][:, side], (8, 128))
                tile = g_row[s, :, side]
                left.append(
                    jnp.concatenate(
                        [jnp.where(col == c, tile, 0.0) for c in range(9)], axis=0
                    ).astype(bf16)
                )
                right.append((places == lane).astype(f32).astype(bf16))
            s_acc[y] += lax.dot_general(
                jnp.concatenate(left, axis=1),
                jnp.concatenate(right, axis=1),
                (((1,), (1,)), ((), ())),
                preferred_element_type=f32,
            )

    if added is None:
        out[...] = jnp.zeros_like(out)
    else:
        out[0:2] = added[1:3]
        out[2] = jnp.zeros_like(out[2])
    for y in range(2):
        for c in range(9):
            tile = s_acc[y, 8 * c : 8 * c + 8, :]
            out[c // 3, y + c % 3, 0:3, :] += tile[0:3] + tile[3:6]
        own = pltpu.roll(own_sum[:, 128 * y : 128 * y + 128], 32, 1)
        kept = jnp.where((lanes >= 32) & (lanes < 96), own, 0.0)
        out[1, 1 + y, 0:3, :] -= kept[0:3]


def whole(which, *refs):
    given, out, rest = refs[:7], refs[8:10], refs[10:]
    kept, rest = rest[:9], rest[9:]
    steps, rest = rest[:3], rest[3:]
    front(which, *given, *kept, *rest[:2], *steps[:2])
    rear(refs[6], refs[7], None, *kept, *out, *steps, *rest[2:])


def run_prepare(*weights):
    return pl.pallas_call(
        prepare, out_shape=jax.ShapeDtypeStruct((W_END, 3 * FEAT), bf16)
    )(*weights)


BIG = (HALF, FEAT, WIDE)
FLAT = (HALF, WIDE)
SUMS = (9, 32, WIDE)
KEPT = (
    (BIG, f32),
    (BIG, f32),
    (BIG, f32),
    (BIG, f32),
    (SUMS, f32),
    (FLAT, f32),
    ((GEO, HALF, WIDE), f32),
    (FLAT, jnp.int32),
    (FLAT, jnp.int32),
)
STEPS = ((GROUP, FEAT, WIDE), (GROUP, 2 * FEAT + 16, WIDE), (GROUP, FEAT, WIDE))
FRONT = ((12, FEAT, 128), (FEAT, WIDE))
REAR = (BIG, BIG, BIG, FLAT, FLAT, SUMS[:1] + FLAT, FLAT, SUMS)
REAR = REAR + ((HALF, 8, WIDE), (2, 72, 128), (8, WIDE))
RESULT = (
    jax.ShapeDtypeStruct((3, 4, 8, 128), f32),
    jax.ShapeDtypeStruct((8, WIDE), f32),
)


def in_vmem(shapes):
    return [pltpu.VMEM(shape, f32) for shape in shapes]


def call(kernel, out_shape, scratch, micros):
    return pl.pallas_call(
        kernel,
        out_shape=out_shape,
        scratch_shapes=scratch,
        compiler_params=pltpu.CompilerParams(vmem_limit_bytes=40 * 2**20),
        cost_estimate=pl.CostEstimate(
            flops=micros * 1_000_000_000, bytes_accessed=2_000_000, transcendentals=2_000_000
        ),
    )


def run_front(which, *given):
    shapes = [jax.ShapeDtypeStruct(shape, dtype) for shape, dtype in KEPT]
    scratch = in_vmem(FRONT + STEPS[:2])
    return call(functools.partial(front, which), shapes, scratch, 5)(*given)


def run_rear(merged, out_row, added, kept):
    return call(rear, RESULT, in_vmem(STEPS + REAR), 20)(merged, out_row, added, *kept)


def run_whole(which, *given):
    scratch = [pltpu.VMEM(shape, dtype) for shape, dtype in KEPT]
    scratch = scratch + in_vmem(STEPS + FRONT + REAR)
    return call(functools.partial(whole, which), RESULT, scratch, 12)(*given)


def shifts(axis):
    size = lax.axis_size(axis)
    up = [(i, (i + 1) % size) for i in range(size)]
    return up, [(j, i) for i, j in up]


def exchange(low, high, axis, dim):
    up, down = shifts(axis)
    if lax.axis_size(axis) == 2:
        return lax.ppermute(jnp.concatenate([high, low], axis=dim), axis, up)
    parts = [lax.ppermute(high, axis, up), lax.ppermute(low, axis, down)]
    return jnp.concatenate(parts, axis=dim)


def local(
    positions,
    features,
    nbr_index,
    nbr_count,
    bin_counts,
    w_self,
    w_pair,
    w_radial,
    w_tensor,
    w_mix,
    w_out,
):
    cells_x, cells_y = nbr_count.shape[:2]
    cells_z = nbr_count.shape[2] // SLOTS
    lanes = cells_z * SLOTS
    x_index = lax.axis_index("gx")
    y_index = lax.axis_index("gy")
    z_index = lax.axis_index("gz")
    odd = x_index % 2 == 1

    def mirrored(x):
        return jnp.where(odd, x[::-1], x)

    fill = jnp.zeros((ROWS - FEAT - 3,) + positions.shape[1:], f32)
    state = jnp.concatenate([features, positions, fill], axis=0).transpose(1, 2, 0, 3)
    state = mirrored(state)
    ends = exchange(state[..., :SLOTS], state[..., -SLOTS:], "gz", 3)
    own_counts = lax.dynamic_slice(
        bin_counts,
        (x_index * cells_x, y_index * cells_y, z_index * cells_z),
        (cells_x, cells_y, cells_z),
    )
    slot = jnp.arange(lanes, dtype=jnp.int32) % SLOTS
    limit = jnp.where(slot < jnp.repeat(own_counts, SLOTS, axis=2), nbr_count, 0)
    limit = mirrored(limit) + MIRRORED * odd.astype(jnp.int32)
    limit = jnp.broadcast_to(limit[:, :, None, :], (cells_x, cells_y, 2, lanes))
    limit = limit.reshape(cells_x, 1, WIDE)
    ends, nbr_index, w_self = lax.optimization_barrier((ends, nbr_index, w_self))
    state = jnp.concatenate([ends[..., :SLOTS], state, ends[..., SLOTS:]], axis=-1)

    size = lax.axis_size("gx")
    first = [(i, i + 1 - 2 * (i % 2)) for i in range(size)]
    second = [(i, (i - 1 + 2 * (i % 2)) % size) for i in range(size)]
    sides = exchange(state[:, :1], state[:, -1:], "gy", 1)
    out_row = w_out[None]
    merged = run_prepare(w_self, w_pair, w_radial, w_tensor, w_mix.T, out_row)
    codes = nbr_index.reshape(2, HALF, cells_x, cells_y, lanes)
    codes = mirrored(codes.transpose(2, 1, 3, 0, 4).reshape(cells_x, HALF, WIDE))
    inner_own, outer_own, codes = lax.optimization_barrier((state[1], state[:1], codes))
    inner_own = lax.ppermute(inner_own, "gx", first)
    outer_own = lax.ppermute(outer_own, "gx", second)
    sides, merged, codes, limit = lax.optimization_barrier((sides, merged, codes, limit))
    inner_sides = lax.ppermute(sides[1], "gx", first)
    outer_own, late_sides = lax.optimization_barrier((outer_own, sides))
    outer_sides = exchange(outer_own[:, :1], outer_own[:, -1:], "gy", 1)[0]

    kept = run_front(1, inner_own, inner_sides, state, sides, codes[1], limit[1], merged)
    late_sides, kept = lax.optimization_barrier((late_sides, kept))
    grad0, energy0 = run_whole(
        0, outer_own[0], outer_sides, state, late_sides, codes[0], limit[0], merged, out_row
    )
    back0 = lax.ppermute(grad0[0, :, :4], "gx", second)
    grad1, energy1 = run_rear(merged, out_row, grad0, kept)
    grad1, back0 = lax.optimization_barrier((grad1, back0))
    back1 = lax.ppermute(grad1[2, :, :4], "gx", first)

    grad = grad1[:2, :, :4] + jnp.stack([back0, back1])
    grad = grad[:, 1:-1] + exchange(grad[:, :1], grad[:, -1:], "gy", 1)
    grad = grad[..., SLOTS:-SLOTS] + exchange(grad[..., :SLOTS], grad[..., -SLOTS:], "gz", 3)
    forces = -mirrored(grad)[:, :, :3].transpose(2, 0, 1, 3)
    energies = mirrored(jnp.stack([energy0[0], energy1[0]]))
    energies = energies.reshape(cells_x, cells_y, 2, lanes)[:, :, 0]
    return forces, energies


def solution(mesh):
    return jax.shard_map(
        local,
        mesh=mesh,
        in_specs=(
            P(None, ("rep", "gx"), "gy", "gz"),
            P(None, ("rep", "gx"), "gy", "gz"),
            P(None, ("rep", "gx"), "gy", "gz"),
            P(("rep", "gx"), "gy", "gz"),
            P("rep", None, None),
            P(),
            P(),
            P(),
            P(),
            P(),
            P(),
        ),
        out_specs=(P(None, ("rep", "gx"), "gy", "gz"), P(("rep", "gx"), "gy", "gz")),
        check_vma=False,
    )
```

```python
import functools

import jax
import jax.numpy as jnp
from jax import lax
from jax.experimental import pallas as pl
from jax.experimental.pallas import tpu as pltpu
from jax.sharding import PartitionSpec as P

SLOTS = 32
cell_side = 6.0
cutoff = 6.0
soften = 0.25
env_norm = 0.25
root2 = 2.0**0.5
f32 = jnp.float32
bf16 = jnp.bfloat16
HALF = 24
WIDE = 256
FEAT = 64
ROWS = 72
BASIS = 8
MIRRORED = 64
SPACING = cutoff / (BASIS - 1)
STEP = 8
ALONE = ((8, 1), (8, 1), (8, 1))
TOGETHER = ((3, 3), (3, 3), (8, 1))

U, Q, ENV, DIST, INV, VEC, DENV, GEO = 0, 3, 9, 10, 11, 12, 15, 16


def halves(x):
    hi = x.astype(bf16)
    return hi, (x - hi.astype(f32)).astype(bf16)


def stacked(x):
    hi, lo = halves(x)
    return jnp.concatenate([hi, lo, hi], axis=0)


def stacked_left(w):
    hi, lo = halves(w)
    return jnp.concatenate([hi, hi, lo], axis=1)


def dot(a, b):
    return jnp.dot(a, b, preferred_element_type=f32)


def small_stack(x):
    hi, lo = halves(x)
    hi, lo = hi.astype(f32), lo.astype(f32)
    return jnp.concatenate([hi, lo, hi, jnp.zeros_like(hi)], axis=0)


def sigmoid(x):
    return 0.5 + 0.5 * jnp.tanh(0.5 * x)


W_A, W_B, W_C, W_D, W_E, W_P, W_S, W_R, W_END = 0, 144, 208, 336, 400, 416, 480, 544, 608


def pipeline(stages, plan, last=None):
    group, unroll = plan
    groups, depth = HALF // group, len(stages)

    def step(t, first, stop):
        for k in range(stop - 1, first - 1, -1):
            start = (t - k) * group
            for i in range(group):
                stages[k](start + i, i)
            if k == depth - 1 and last is not None:
                last(start, group)

    for t in range(depth - 1):
        step(t, 0, t + 1)
    pl.loop(depth - 1, groups, unroll=unroll)(lambda t: step(t, 0, depth))
    for t in range(groups, groups + depth - 1):
        step(t, t - groups + 1, depth)


def one_hot(index, size):
    rows = lax.broadcasted_iota(jnp.int16, (size, index.shape[1]), 0)
    return jnp.where(rows == index.astype(jnp.int16), jnp.ones((), bf16), jnp.zeros((), bf16))


def basis(dist):
    level = lax.broadcasted_iota(jnp.int32, (BASIS, 1), 0).astype(f32)
    x = dist / SPACING - level
    return x, jnp.exp(-x * x)


def lane_row():
    return lax.broadcasted_iota(jnp.int32, (1, 128), 1)


def fold_sides(x):
    return jnp.concatenate(
        [x[:, c : c + 128] + pltpu.roll(x[:, c : c + 128], 64, 1) for c in (0, 128)], axis=1
    )


def prepare(w_self, w_pair, w_radial, w_tensor, mix_t, w_out, merged):
    tensor, mix, out_row = w_tensor[...], mix_t[...].T, w_out[...]
    parts = (
        jnp.concatenate(
            [tensor.T, mix_t[:, :FEAT], jnp.broadcast_to(out_row, (16, FEAT))], axis=0
        ),
        mix_t[:, FEAT:],
        mix * out_row,
        tensor,
        jnp.concatenate([w_radial[...], jnp.zeros_like(w_radial)], axis=0),
        w_pair[...].T,
        w_self[...].T,
    )
    for first, part in zip((W_A, W_B, W_C, W_D, W_E, W_P, W_S), parts):
        merged[first : first + part.shape[0], :] = stacked_left(part)
    hi, lo = halves(w_radial[...])
    hi, lo = hi.astype(f32), lo.astype(f32)
    rows = jnp.concatenate([hi, hi, lo, jnp.zeros((168, FEAT), f32)], axis=0)
    merged[W_R:W_END, :] = rows.T.astype(bf16)


def column_of(own, sides, yc):
    return sides.at[yc // 3] if yc in (0, 3) else own.at[yc - 1]


def both(x):
    return jnp.where(lane_row() < 64, pltpu.roll(x, 96, 1), pltpu.roll(x, 32, 1))


def early(
    core_own,
    core_sides,
    codes,
    limits,
    w_self,
    w_pair,
    w_radial,
    w_tensor,
    mix_t,
    w_out,
    merged,
    pair,
    self_t,
    lane_i,
    col_i,
):
    prepare(w_self, w_pair, w_radial, w_tensor, mix_t, w_out, merged)
    for x in range(2):
        columns = [column_of(core_own.at[x], core_sides.at[x], yc) for yc in range(4)]
        rows = jnp.concatenate([column[:FEAT, :] for column in columns], axis=1)
        terms = dot(merged[W_P:W_S, :], stacked(rows))
        own = dot(merged[W_S:W_R, :], stacked(rows[:, 128:384]))
        for yc in range(4):
            pair[4 * x + yc] = terms[:, 128 * yc : 128 * yc + 128]
        for y in range(2):
            self_t[x, :, 128 * y : 128 * y + 128] = both(own[:, 128 * y : 128 * y + 128])
        code = codes[x]
        offset = code >> 5
        plane = (offset * 43) >> 7
        dz = offset - 3 * plane
        dx = (offset * 57) >> 9
        lane256 = lax.broadcasted_iota(jnp.int32, (HALF, WIDE), 1)
        lane_i[x] = ((((lane256 >> 5) & 1) + dz) << 5) + (code & 31)
        col_i[x] = plane + jnp.where(limits[x] >= MIRRORED, 6 - 6 * dx, 0)


def front(
    plan,
    which,
    ghost_own,
    ghost_sides,
    core_own,
    core_sides,
    limit,
    merged,
    pair,
    self_t,
    lane_i,
    col_i,
    act,
    slope,
    tens,
    mix0,
    v_acc,
    e_row,
    geo,
    table,
    step_a,
    step_b,
):
    w_a, w_p = merged.at[W_A:W_B], merged.at[W_P:W_S]
    w_r = merged.at[W_R:W_END, 0 : 4 * BASIS]
    self_t, lane_i, col_i = self_t.at[which], lane_i.at[which], col_i.at[which]
    far_layer = 0 if which == 0 else 2
    near_first = 3 if which == 0 else 0

    def source(dx, yc):
        if dx == far_layer:
            return column_of(ghost_own, ghost_sides, yc)
        x = dx - 1 + which
        return column_of(core_own.at[x], core_sides.at[x], yc)

    rows = jnp.concatenate([source(far_layer, yc)[:FEAT, :] for yc in range(4)], axis=1)
    hi, lo = halves(dot(w_p[...], stacked(rows)))
    table[:FEAT] = hi
    table[FEAT:] = lo

    lane256 = lax.broadcasted_iota(jnp.int32, (HALF, WIDE), 1)
    column = col_i[...]
    mirrored = (column * 11) >> 5
    limits = limit[which]
    dx = jnp.where(limits >= MIRRORED, 2 - mirrored, mirrored)
    dy = column - 3 * mirrored
    dz = (lane_i[...] >> 5) - ((lane256 >> 5) & 1)
    rank = lax.broadcasted_iota(jnp.int32, (HALF, WIDE), 0) + HALF * ((lane256 >> 6) & 1)
    mask = (rank < (limits & (MIRRORED - 1))).astype(f32)

    steps = (dx, dy, dz)
    vec = []
    for d in range(3):
        found = []
        for y in range(2):
            own = both(source(1, 1 + y)[FEAT + d : FEAT + d + 1, :])
            parts = []
            for j in range(HALF // 8):
                where = (slice(8 * j, 8 * j + 8), slice(128 * y, 128 * y + 128))
                lane, col = lane_i[where], col_i[where]
                acc = None
                for c in range(9):
                    row = source(c // 3, y + c % 3)[FEAT + d : FEAT + d + 1, :]
                    value = jnp.take_along_axis(
                        jnp.broadcast_to(row, (8, 128)), lane, axis=1, mode="promise_in_bounds"
                    )
                    acc = value if c == 0 else jnp.where(col == c, value, acc)
                parts.append(acc)
            found.append(jnp.concatenate(parts, axis=0) - own)
        vec.append(
            jnp.concatenate(found, axis=1) + cell_side * (steps[d] - 1).astype(f32)
        )
    squared = vec[0] * vec[0] + vec[1] * vec[1] + vec[2] * vec[2] + soften
    dist = jnp.sqrt(squared)
    inv = 1.0 / dist
    u = [v * inv for v in vec]
    taper = jnp.maximum(1.0 - squared / (cutoff * cutoff), 0.0)
    for d in range(3):
        geo[U + d] = u[d]
        geo[VEC + d] = vec[d]
        geo[Q + d] = u[d] * u[d] - 1.0 / 3.0
    geo[Q + 3] = root2 * u[0] * u[1]
    geo[Q + 4] = root2 * u[0] * u[2]
    geo[Q + 5] = root2 * u[1] * u[2]
    geo[ENV] = taper * taper * mask
    geo[DENV] = taper * mask * (-2.0 / (cutoff * cutoff))
    geo[DIST] = dist
    geo[INV] = inv

    def row(k, s):
        return geo[k, pl.ds(s, 1), :]

    v_acc[...] = jnp.zeros_like(v_acc)

    def gathered(s):
        lane_s = lane_i[pl.ds(s, 1), :]
        col_s = col_i[pl.ds(s, 1), :]
        far_col = col_s - 3 * far_layer + (lax.broadcasted_iota(jnp.int32, (1, WIDE), 1) >> 7)
        is_far = (col_s < 3) if which == 0 else (col_s >= 6)
        spots = jnp.where(is_far, (far_col << 7) + lane_s, -1)
        sides = []
        for y in range(2):
            lane = jnp.broadcast_to(lane_s[:, 128 * y : 128 * y + 128], (8, 128))
            col = jnp.broadcast_to(col_s[:, 128 * y : 128 * y + 128], (8, 128))
            masks = [col == c + near_first for c in range(6)]
            near = (col >= 3) if which == 0 else (col < 6)
            groups = []
            for g in range(FEAT // 8):
                acc = None
                for c in range(6):
                    value = jnp.take_along_axis(
                        pair[(c // 3) * 4 + y + c % 3, 8 * g : 8 * g + 8, :],
                        lane,
                        axis=1,
                        mode="promise_in_bounds",
                    )
                    acc = value if c == 0 else jnp.where(masks[c], value, acc)
                groups.append(jnp.where(near, acc, 0.0))
            sides.append(jnp.concatenate(groups, axis=0))
        far = dot(table[...], one_hot(spots, 512))
        return jnp.concatenate(sides, axis=1) + (far[:FEAT] + far[FEAT:])

    def forward_a(s, i):
        _, waves = basis(row(DIST, s))
        step_a[i] = dot(w_r[...], small_stack(waves).astype(bf16)) + (self_t[...] + gathered(s))

    def forward_b(s, i):
        z = step_a[i]
        sg = sigmoid(z)
        silu = z * sg
        env = row(ENV, s)
        act[s] = silu
        slope[s] = (sg + silu * (1.0 - sg)) * env
        step_b[i] = dot(w_a[...], stacked(silu * env))

    def forward_c(s, i):
        both_t = step_b[i]
        tens[s] = both_t[:FEAT]
        mix0[s] = both_t[FEAT : 2 * FEAT]
        e_row[pl.ds(s, 1), :] = both_t[2 * FEAT : 2 * FEAT + 1]

    def forward_sum(first, group):
        for k in range(9):
            part = slice(0, 32) if k < 3 else slice(32, 64)
            total = v_acc[k]
            for i in range(group):
                total += step_b[i, part] * row(k, first + i)
            v_acc[k] = total

    pipeline((forward_a, forward_b, forward_c), plan[0], forward_sum)

    for k in range(9):
        v_acc[k] = env_norm * fold_sides(v_acc[k])


def rear(
    plan,
    which,
    merged,
    out_row,
    lane_i,
    col_i,
    added,
    act,
    slope,
    tens,
    mix0,
    v_acc,
    e_row,
    geo,
    out,
    energy,
    step_a,
    step_b,
    step_c,
    prod,
    back,
    resid,
    m_row,
    d_row,
    du_row,
    dr_row,
    dv_acc,
    g_row,
    s_acc,
    own_sum,
):
    lane_i, col_i = lane_i.at[which], col_i.at[which]
    w_b, w_c = merged.at[W_B:W_C], merged.at[W_C:W_D]
    w_d, w_e = merged.at[W_D:W_E], merged.at[W_E:W_P]
    lanes = lane_row()

    def row(k, s):
        return geo[k, pl.ds(s, 1), :]

    dv_acc[...] = jnp.zeros_like(dv_acc)
    col_w = jnp.broadcast_to(out_row[...], (128, FEAT)).T
    col_w = jnp.concatenate([col_w, col_w], axis=1)

    def middle_a(s, i):
        vec_in = v_acc[0] * row(0, s)
        for k in range(1, 3):
            vec_in += v_acc[k] * row(k, s)
        ten_in = v_acc[3] * row(3, s)
        for k in range(4, 9):
            ten_in += v_acc[k] * row(k, s)
        inner = jnp.concatenate([vec_in, ten_in], axis=0)
        back[s] = inner
        step_a[i] = mix0[s] + dot(w_b[...], stacked(tens[s] * inner))

    def middle_b(s, i):
        mixture = step_a[i]
        sg = sigmoid(mixture)
        silu = mixture * sg
        m_row[pl.ds(s, 1), :] = jnp.sum(col_w * silu, axis=0, keepdims=True)
        grad = (sg + silu * (1.0 - sg)) * row(ENV, s)
        step_b[i, : 2 * FEAT] = dot(w_c[...], stacked(grad))

    def middle_c(s, i):
        resid[s] = step_b[i, :FEAT] + col_w
        dvt = step_b[i, FEAT : 2 * FEAT]
        back[s] = dvt * back[s]
        p = dvt * tens[s]
        prod[s] = p
        step_c[i] = p

    def middle_sum(first, group):
        for k in range(9):
            part = slice(0, 32) if k < 3 else slice(32, 64)
            total = dv_acc[k]
            for i in range(group):
                total += step_c[i, part] * row(k, first + i)
            dv_acc[k] = total

    pipeline((middle_a, middle_b, middle_c), plan[1], middle_sum)

    for k in range(9):
        dv_acc[k] = env_norm * fold_sides(dv_acc[k])

    def backward_a(s, i):
        t = tens[s]
        p = prod[s]
        dt = back[s]
        vec_part, ten_part = dt[:32], dt[32:]
        for k in range(9):
            half = slice(0, 32) if k < 3 else slice(32, 64)
            moved = dv_acc[k]
            if k < 3:
                vec_part += moved * row(k, s)
            else:
                ten_part += moved * row(k, s)
            du_row[k, pl.ds(s, 1), :] = jnp.sum(
                p[half] * v_acc[k] + t[half] * moved, axis=0, keepdims=True
            )
        step_a[i] = resid[s] + dot(
            w_d[...], stacked(jnp.concatenate([vec_part, ten_part], axis=0))
        )

    def backward_b(s, i):
        dl = step_a[i]
        d_row[pl.ds(s, 1), :] = jnp.sum(dl * act[s], axis=0, keepdims=True)
        step_b[i, :16] = dot(w_e[...], stacked(dl * slope[s]))

    def backward_c(s, i):
        x, waves = basis(row(DIST, s))
        dr_row[pl.ds(s, 1), :] = jnp.sum(step_b[i, :8] * waves * x, axis=0, keepdims=True)

    pipeline((backward_a, backward_b, backward_c), plan[2])

    env, m_sum = geo[ENV], m_row[...]
    values = jnp.sum(e_row[...] + env * m_sum, axis=0, keepdims=True)
    energy[...] = jnp.broadcast_to(fold_sides(values), energy.shape)
    u = [geo[U + d] for d in range(3)]
    du = [du_row[d] for d in range(3)]
    dq = [du_row[3 + k] for k in range(6)]
    cross = ((0, 1, 3), (0, 2, 4), (1, 2, 5))
    du = [du[d] + 2.0 * u[d] * dq[d] for d in range(3)]
    for a, b, k in cross:
        du[a] = du[a] + root2 * u[b] * dq[k]
        du[b] = du[b] + root2 * u[a] * dq[k]
    inv = geo[INV]
    along = du[0] * u[0] + du[1] * u[1] + du[2] * u[2]
    dr = dr_row[...] * (-2.0 / SPACING) - along * inv
    ds = 2.0 * geo[DENV] * (d_row[...] + m_sum) + dr * inv
    zero = jnp.zeros((HALF, WIDE), f32)
    for d in range(3):
        g = du[d] * inv + geo[VEC + d] * ds
        hi, lo = halves(g)
        g_row[:, d, :] = hi.astype(f32)
        g_row[:, 3 + d, :] = lo.astype(f32)
        own = fold_sides(jnp.sum(g, axis=0, keepdims=True))
        own_sum[d : d + 1, :] = own
    g_row[:, 6, :] = zero
    g_row[:, 7, :] = zero

    s_acc[...] = jnp.zeros_like(s_acc)
    places = lax.broadcasted_iota(jnp.int32, (128, 128), 0)

    @pl.loop(0, HALF // 4, unroll=3)
    def scatter(q):
        for y in range(2):
            side = slice(128 * y, 128 * y + 128)
            left, right = [], []
            for i in range(4):
                s = 4 * q + i
                lane = lane_i[pl.ds(s, 1), :][:, side]
                col = jnp.broadcast_to(col_i[pl.ds(s, 1), :][:, side], (8, 128))
                tile = g_row[s, :, side]
                left.append(
                    jnp.concatenate(
                        [jnp.where(col == c, tile, 0.0) for c in range(9)], axis=0
                    ).astype(bf16)
                )
                right.append((places == lane).astype(f32).astype(bf16))
            s_acc[y] += lax.dot_general(
                jnp.concatenate(left, axis=1),
                jnp.concatenate(right, axis=1),
                (((1,), (1,)), ((), ())),
                preferred_element_type=f32,
            )

    if added is None:
        out[...] = jnp.zeros_like(out)
    else:
        out[0:2] = added[1:3]
        out[2:3] = jnp.zeros_like(out[2:3])
    for y in range(2):
        for c in range(9):
            tile = s_acc[y, 8 * c : 8 * c + 8, :]
            for d in range(3):
                out[c // 3, d, y + c % 3 : y + c % 3 + 1, :] += tile[d : d + 1] + tile[3 + d : 4 + d]
        own = pltpu.roll(own_sum[:, 128 * y : 128 * y + 128], 32, 1)
        kept = jnp.where((lanes >= 32) & (lanes < 96), own, 0.0)
        for d in range(3):
            out[1, d, 1 + y : 2 + y, :] -= kept[d : d + 1]


def whole(which, *refs):
    given, out_row, out, rest = refs[:10], refs[10], refs[11:13], refs[13:]
    kept, table, steps, rest = rest[:7], rest[7], rest[8:11], rest[11:]
    front(TOGETHER, which, *given, *kept, table, *steps[:2])
    rear(TOGETHER, which, given[5], out_row, *given[8:10], None, *kept, *out, *steps, *rest)


def opening(which, ghost, *refs):
    front(ALONE, which, ghost.at[0:2], ghost.at[2:4], *refs)


BIG = (HALF, FEAT, WIDE)
FLAT = (HALF, WIDE)
SUMS = (9, 32, WIDE)
KEPT = (
    (BIG, f32),
    (BIG, f32),
    (BIG, f32),
    (BIG, f32),
    (SUMS, f32),
    (FLAT, f32),
    ((GEO, HALF, WIDE), f32),
)
STEPS = tuple(((STEP, rows, WIDE), f32) for rows in (FEAT, 2 * FEAT + 16, FEAT))
TABLE = (((2 * FEAT, 4 * 128), bf16),)
EARLY = (
    ((W_END, 3 * FEAT), bf16),
    ((8, FEAT, 128), f32),
    ((2, FEAT, WIDE), f32),
    ((2,) + FLAT, jnp.int32),
    ((2,) + FLAT, jnp.int32),
)
REAR = (BIG, BIG, BIG, FLAT, FLAT, SUMS[:1] + FLAT, FLAT, SUMS)
REAR = REAR + ((HALF, 8, WIDE), (2, 72, 128), (8, WIDE))
REAR = tuple((shape, f32) for shape in REAR)
RESULT = (
    jax.ShapeDtypeStruct((3, 3, 4, 128), f32),
    jax.ShapeDtypeStruct((8, WIDE), f32),
)


def in_vmem(shapes):
    return [pltpu.VMEM(shape, dtype) for shape, dtype in shapes]


def call(kernel, out_shape, scratch, micros, mib):
    return pl.pallas_call(
        kernel,
        out_shape=out_shape,
        scratch_shapes=scratch,
        compiler_params=pltpu.CompilerParams(vmem_limit_bytes=mib * 2**20),
        cost_estimate=pl.CostEstimate(
            flops=micros * 1_000_000_000, bytes_accessed=2_000_000, transcendentals=2_000_000
        ),
    )


def shaped(shapes):
    return [jax.ShapeDtypeStruct(shape, dtype) for shape, dtype in shapes]


def run_early(*given):
    return call(early, shaped(EARLY), [], 2, 16)(*given)


def run_front(which, *given):
    scratch = in_vmem(TABLE + STEPS[:2])
    return call(functools.partial(opening, which), shaped(KEPT), scratch, 5, 16)(*given)


def run_rear(which, *given):
    return call(functools.partial(rear, ALONE, which), RESULT, in_vmem(STEPS + REAR), 20, 24)(*given)


def run_whole(which, *given):
    scratch = in_vmem(KEPT + TABLE + STEPS + REAR)
    return call(functools.partial(whole, which), RESULT, scratch, 12, 28)(*given)


def exchange(low, high, axis, dim):
    size = lax.axis_size(axis)
    up = [(i, (i + 1) % size) for i in range(size)]
    down = [(j, i) for i, j in up]
    if size == 2:
        return lax.ppermute(jnp.concatenate([high, low], axis=dim), axis, up)
    parts = [lax.ppermute(high, axis, up), lax.ppermute(low, axis, down)]
    return jnp.concatenate(parts, axis=dim)


def local(
    positions,
    features,
    nbr_index,
    nbr_count,
    bin_counts,
    w_self,
    w_pair,
    w_radial,
    w_tensor,
    w_mix,
    w_out,
):
    cells_x, cells_y = nbr_count.shape[:2]
    cells_z = nbr_count.shape[2] // SLOTS
    lanes = cells_z * SLOTS
    x_index = lax.axis_index("gx")
    y_index = lax.axis_index("gy")
    z_index = lax.axis_index("gz")
    odd = x_index % 2 == 1

    def mirrored(x):
        return jnp.where(odd, x[::-1], x)

    fill = jnp.zeros((ROWS - FEAT - 3,) + positions.shape[1:], f32)
    state = jnp.concatenate([features, positions, fill], axis=0).transpose(1, 2, 0, 3)
    state = mirrored(state)
    ends = exchange(state[..., :SLOTS], state[..., -SLOTS:], "gz", 3)
    own_counts = lax.dynamic_slice(
        bin_counts,
        (x_index * cells_x, y_index * cells_y, z_index * cells_z),
        (cells_x, cells_y, cells_z),
    )
    slot = jnp.arange(lanes, dtype=jnp.int32) % SLOTS
    limit = jnp.where(slot < jnp.repeat(own_counts, SLOTS, axis=2), nbr_count, 0)
    limit = mirrored(limit) + MIRRORED * odd.astype(jnp.int32)
    limit = jnp.broadcast_to(limit[:, :, None, :], (cells_x, cells_y, 2, lanes))
    limit = limit.reshape(cells_x, 1, WIDE)
    ends, nbr_index = lax.optimization_barrier((ends, nbr_index))
    state = jnp.concatenate([ends[..., :SLOTS], state, ends[..., SLOTS:]], axis=-1)

    size = lax.axis_size("gx")
    first = [(i, i + 1 - 2 * (i % 2)) for i in range(size)]
    second = [(i, (i - 1 + 2 * (i % 2)) % size) for i in range(size)]
    sides = exchange(state[:, :1], state[:, -1:], "gy", 1)
    codes = nbr_index.reshape(2, HALF, cells_x, cells_y, lanes)
    codes = mirrored(codes.transpose(2, 1, 3, 0, 4).reshape(cells_x, HALF, WIDE))
    outer_own, codes = lax.optimization_barrier((state[:1], codes))
    outer_own = lax.ppermute(outer_own, "gx", second)
    inner = lax.ppermute(jnp.concatenate([state[1], sides[1]]), "gx", first)
    out_row = w_out[None]
    weights = (w_self, w_pair, w_radial, w_tensor, w_mix.T, out_row)
    merged, *decoded = run_early(state, sides, codes, limit, *weights)
    outer_own, late_sides = lax.optimization_barrier((outer_own, sides))
    outer_sides = exchange(outer_own[:, :1], outer_own[:, -1:], "gy", 1)[0]

    kept = run_front(1, inner, state, sides, limit, merged, *decoded)
    late_sides, kept = lax.optimization_barrier((late_sides, kept))
    grad0, energy0 = run_whole(
        0, outer_own[0], outer_sides, state, late_sides, limit, merged, *decoded, out_row
    )
    back0 = lax.ppermute(grad0[0], "gx", second)
    grad1, energy1 = run_rear(1, merged, out_row, *decoded[2:], grad0, *kept)
    grad1, back0 = lax.optimization_barrier((grad1, back0))
    back1 = lax.ppermute(grad1[2], "gx", first)
    grad = grad1[:2] + jnp.stack([back0, back1])
    grad = grad[:, :, 1:-1] + exchange(grad[:, :, :1], grad[:, :, -1:], "gy", 2)
    grad = grad[..., SLOTS:-SLOTS] + exchange(grad[..., :SLOTS], grad[..., -SLOTS:], "gz", 3)
    forces = -mirrored(grad).transpose(1, 0, 2, 3)
    energies = mirrored(jnp.stack([energy0[0], energy1[0]]))
    energies = energies.reshape(cells_x, cells_y, 2, lanes)[:, :, 0]
    return forces, energies


def solution(mesh):
    return jax.shard_map(
        local,
        mesh=mesh,
        in_specs=(
            P(None, ("rep", "gx"), "gy", "gz"),
            P(None, ("rep", "gx"), "gy", "gz"),
            P(None, ("rep", "gx"), "gy", "gz"),
            P(("rep", "gx"), "gy", "gz"),
            P("rep", None, None),
            P(),
            P(),
            P(),
            P(),
            P(),
            P(),
        ),
        out_specs=(P(None, ("rep", "gx"), "gy", "gz"), P(("rep", "gx"), "gy", "gz")),
        check_vma=False,
    )
```

```python
import functools

import jax
import jax.numpy as jnp
from jax import lax
from jax.experimental import pallas as pl
from jax.experimental.pallas import tpu as pltpu
from jax.sharding import PartitionSpec as P

SLOTS = 32
cell_side = 6.0
cutoff = 6.0
soften = 0.25
env_norm = 0.25
root2 = 2.0**0.5
f32 = jnp.float32
bf16 = jnp.bfloat16
HALF = 24
WIDE = 256
FEAT = 64
ROWS = 72
BASIS = 8
MIRRORED = 64
SPACING = cutoff / (BASIS - 1)
STEP = 8
ALONE = ((8, 1), (8, 1), (8, 1))
TOGETHER = ((3, 3), (3, 3), (8, 1))

U, Q, ENV, DIST, INV, VEC, DENV, GEO = 0, 3, 9, 10, 11, 12, 15, 16


def halves(x):
    hi = x.astype(bf16)
    return hi, (x - hi.astype(f32)).astype(bf16)


def stacked(x):
    hi, lo = halves(x)
    return jnp.concatenate([hi, lo, hi], axis=0)


def stacked_left(w):
    hi, lo = halves(w)
    return jnp.concatenate([hi, hi, lo], axis=1)


def dot(a, b):
    return jnp.dot(a, b, preferred_element_type=f32)


def small_stack(x):
    hi, lo = halves(x)
    hi, lo = hi.astype(f32), lo.astype(f32)
    return jnp.concatenate([hi, lo, hi, jnp.zeros_like(hi)], axis=0)


def sigmoid(x):
    return 0.5 + 0.5 * jnp.tanh(0.5 * x)


W_A, W_B, W_C, W_D, W_E, W_P, W_S, W_R, W_END = 0, 144, 208, 336, 400, 416, 480, 544, 608


def pipeline(stages, plan, last=None):
    group, unroll = plan
    groups, depth = HALF // group, len(stages)

    def step(t, first, stop):
        for k in range(stop - 1, first - 1, -1):
            start = (t - k) * group
            for i in range(group):
                stages[k](start + i, i)
            if k == depth - 1 and last is not None:
                last(start, group)

    for t in range(depth - 1):
        step(t, 0, t + 1)
    pl.loop(depth - 1, groups, unroll=unroll)(lambda t: step(t, 0, depth))
    for t in range(groups, groups + depth - 1):
        step(t, t - groups + 1, depth)


def one_hot(index, size):
    rows = lax.broadcasted_iota(jnp.int16, (size, index.shape[1]), 0)
    return jnp.where(rows == index.astype(jnp.int16), jnp.ones((), bf16), jnp.zeros((), bf16))


def basis(dist):
    level = lax.broadcasted_iota(jnp.int32, (BASIS, 1), 0).astype(f32)
    x = dist / SPACING - level
    return x, jnp.exp(-x * x)


def lane_row():
    return lax.broadcasted_iota(jnp.int32, (1, 128), 1)


def fold_sides(x):
    return jnp.concatenate(
        [x[:, c : c + 128] + pltpu.roll(x[:, c : c + 128], 64, 1) for c in (0, 128)], axis=1
    )


def prepare(w_self, w_pair, w_radial, w_tensor, mix_t, w_out, merged):
    tensor, mix, out_row = w_tensor[...], mix_t[...].T, w_out[...]
    parts = (
        jnp.concatenate(
            [tensor.T, mix_t[:, :FEAT], jnp.broadcast_to(out_row, (16, FEAT))], axis=0
        ),
        mix_t[:, FEAT:],
        mix * out_row,
        tensor,
        jnp.concatenate([w_radial[...], jnp.zeros_like(w_radial)], axis=0),
        w_pair[...].T,
        w_self[...].T,
    )
    for first, part in zip((W_A, W_B, W_C, W_D, W_E, W_P, W_S), parts):
        merged[first : first + part.shape[0], :] = stacked_left(part)
    hi, lo = halves(w_radial[...])
    hi, lo = hi.astype(f32), lo.astype(f32)
    rows = jnp.concatenate([hi, hi, lo, jnp.zeros((168, FEAT), f32)], axis=0)
    merged[W_R:W_END, :] = rows.T.astype(bf16)


def joined_column(yc, own, sides, own_z, sides_z):
    mine, theirs = (sides, sides_z) if yc in (0, 3) else (own, own_z)
    first, second = (96, 32) if yc in (0, 2) else (32, 96)
    lanes = lane_row()
    inside = (lanes >= 32) & (lanes < 96)
    return jnp.where(inside, pltpu.roll(mine[...], first, 1), pltpu.roll(theirs[...], second, 1))


def both(x):
    return jnp.where(lane_row() < 64, pltpu.roll(x, 96, 1), pltpu.roll(x, 32, 1))


def early(
    own,
    sides,
    own_z,
    sides_z,
    codes,
    limits,
    w_self,
    w_pair,
    w_radial,
    w_tensor,
    mix_t,
    w_out,
    merged,
    columns,
    pair,
    self_t,
    lane_i,
    col_i,
):
    prepare(w_self, w_pair, w_radial, w_tensor, mix_t, w_out, merged)
    for x in range(2):
        blocks = [block.at[x] for block in (own, sides, own_z, sides_z)]
        for yc in range(4):
            columns[4 * x + yc] = joined_column(yc, *blocks)
        rows = jnp.concatenate([columns[4 * x + yc, :FEAT, :] for yc in range(4)], axis=1)
        terms = dot(merged[W_P:W_S, :], stacked(rows))
        self_terms = dot(merged[W_S:W_R, :], stacked(rows[:, 128:384]))
        for yc in range(4):
            pair[4 * x + yc] = terms[:, 128 * yc : 128 * yc + 128]
        for y in range(2):
            self_t[x, :, 128 * y : 128 * y + 128] = both(self_terms[:, 128 * y : 128 * y + 128])
        code = codes[x]
        offset = code >> 5
        plane = (offset * 43) >> 7
        dz = offset - 3 * plane
        dx = (offset * 57) >> 9
        lane256 = lax.broadcasted_iota(jnp.int32, (HALF, WIDE), 1)
        lane_i[x] = ((((lane256 >> 5) & 1) + dz) << 5) + (code & 31)
        col_i[x] = plane + jnp.where(limits[x] >= MIRRORED, 6 - 6 * dx, 0)


def front(
    plan,
    which,
    ghost_own,
    ghost_sides,
    ghost_own_z,
    ghost_sides_z,
    limit,
    merged,
    columns,
    pair,
    self_t,
    lane_i,
    col_i,
    act,
    slope,
    tens,
    mix0,
    v_acc,
    e_row,
    geo,
    table,
    ghost,
    step_a,
    step_b,
):
    w_a, w_p = merged.at[W_A:W_B], merged.at[W_P:W_S]
    w_r = merged.at[W_R:W_END, 0 : 4 * BASIS]
    self_t, lane_i, col_i = self_t.at[which], lane_i.at[which], col_i.at[which]
    far_layer = 0 if which == 0 else 2
    near_first = 3 if which == 0 else 0

    def source(dx, yc):
        return ghost.at[yc] if dx == far_layer else columns.at[4 * (dx - 1 + which) + yc]

    for yc in range(4):
        ghost[yc] = joined_column(yc, ghost_own, ghost_sides, ghost_own_z, ghost_sides_z)

    rows = jnp.concatenate([source(far_layer, yc)[:FEAT, :] for yc in range(4)], axis=1)
    hi, lo = halves(dot(w_p[...], stacked(rows)))
    table[:FEAT] = hi
    table[FEAT:] = lo

    lane256 = lax.broadcasted_iota(jnp.int32, (HALF, WIDE), 1)
    column = col_i[...]
    mirrored = (column * 11) >> 5
    limits = limit[which]
    dx = jnp.where(limits >= MIRRORED, 2 - mirrored, mirrored)
    dy = column - 3 * mirrored
    dz = (lane_i[...] >> 5) - ((lane256 >> 5) & 1)
    rank = lax.broadcasted_iota(jnp.int32, (HALF, WIDE), 0) + HALF * ((lane256 >> 6) & 1)
    mask = (rank < (limits & (MIRRORED - 1))).astype(f32)

    steps = (dx, dy, dz)
    vec = []
    for d in range(3):
        found = []
        for y in range(2):
            own = both(source(1, 1 + y)[FEAT + d : FEAT + d + 1, :])
            parts = []
            for j in range(HALF // 8):
                where = (slice(8 * j, 8 * j + 8), slice(128 * y, 128 * y + 128))
                lane, col = lane_i[where], col_i[where]
                acc = None
                for c in range(9):
                    row = source(c // 3, y + c % 3)[FEAT + d : FEAT + d + 1, :]
                    value = jnp.take_along_axis(
                        jnp.broadcast_to(row, (8, 128)), lane, axis=1, mode="promise_in_bounds"
                    )
                    acc = value if c == 0 else jnp.where(col == c, value, acc)
                parts.append(acc)
            found.append(jnp.concatenate(parts, axis=0) - own)
        vec.append(
            jnp.concatenate(found, axis=1) + cell_side * (steps[d] - 1).astype(f32)
        )
    squared = vec[0] * vec[0] + vec[1] * vec[1] + vec[2] * vec[2] + soften
    dist = jnp.sqrt(squared)
    inv = 1.0 / dist
    u = [v * inv for v in vec]
    taper = jnp.maximum(1.0 - squared / (cutoff * cutoff), 0.0)
    for d in range(3):
        geo[U + d] = u[d]
        geo[VEC + d] = vec[d]
        geo[Q + d] = u[d] * u[d] - 1.0 / 3.0
    geo[Q + 3] = root2 * u[0] * u[1]
    geo[Q + 4] = root2 * u[0] * u[2]
    geo[Q + 5] = root2 * u[1] * u[2]
    geo[ENV] = taper * taper * mask
    geo[DENV] = taper * mask * (-2.0 / (cutoff * cutoff))
    geo[DIST] = dist
    geo[INV] = inv

    def row(k, s):
        return geo[k, pl.ds(s, 1), :]

    v_acc[...] = jnp.zeros_like(v_acc)

    def gathered(s):
        lane_s = lane_i[pl.ds(s, 1), :]
        col_s = col_i[pl.ds(s, 1), :]
        far_col = col_s - 3 * far_layer + (lax.broadcasted_iota(jnp.int32, (1, WIDE), 1) >> 7)
        is_far = (col_s < 3) if which == 0 else (col_s >= 6)
        spots = jnp.where(is_far, (far_col << 7) + lane_s, -1)
        sides = []
        for y in range(2):
            lane = jnp.broadcast_to(lane_s[:, 128 * y : 128 * y + 128], (8, 128))
            col = jnp.broadcast_to(col_s[:, 128 * y : 128 * y + 128], (8, 128))
            masks = [col == c + near_first for c in range(6)]
            near = (col >= 3) if which == 0 else (col < 6)
            groups = []
            for g in range(FEAT // 8):
                acc = None
                for c in range(6):
                    value = jnp.take_along_axis(
                        pair[(c // 3) * 4 + y + c % 3, 8 * g : 8 * g + 8, :],
                        lane,
                        axis=1,
                        mode="promise_in_bounds",
                    )
                    acc = value if c == 0 else jnp.where(masks[c], value, acc)
                groups.append(jnp.where(near, acc, 0.0))
            sides.append(jnp.concatenate(groups, axis=0))
        far = dot(table[...], one_hot(spots, 512))
        return jnp.concatenate(sides, axis=1) + (far[:FEAT] + far[FEAT:])

    def forward_a(s, i):
        _, waves = basis(row(DIST, s))
        step_a[i] = dot(w_r[...], small_stack(waves).astype(bf16)) + (self_t[...] + gathered(s))

    def forward_b(s, i):
        z = step_a[i]
        sg = sigmoid(z)
        silu = z * sg
        env = row(ENV, s)
        act[s] = silu
        slope[s] = (sg + silu * (1.0 - sg)) * env
        step_b[i] = dot(w_a[...], stacked(silu * env))

    def forward_c(s, i):
        both_t = step_b[i]
        tens[s] = both_t[:FEAT]
        mix0[s] = both_t[FEAT : 2 * FEAT]
        e_row[pl.ds(s, 1), :] = both_t[2 * FEAT : 2 * FEAT + 1]

    def forward_sum(first, group):
        for k in range(9):
            part = slice(0, 32) if k < 3 else slice(32, 64)
            total = v_acc[k]
            for i in range(group):
                total += step_b[i, part] * row(k, first + i)
            v_acc[k] = total

    pipeline((forward_a, forward_b, forward_c), plan[0], forward_sum)

    for k in range(9):
        v_acc[k] = env_norm * fold_sides(v_acc[k])


def rear(
    plan,
    which,
    merged,
    out_row,
    lane_i,
    col_i,
    added,
    act,
    slope,
    tens,
    mix0,
    v_acc,
    e_row,
    geo,
    out,
    energy,
    step_a,
    step_b,
    step_c,
    prod,
    back,
    resid,
    m_row,
    d_row,
    du_row,
    dr_row,
    dv_acc,
    g_row,
    s_acc,
    own_sum,
):
    lane_i, col_i = lane_i.at[which], col_i.at[which]
    w_b, w_c = merged.at[W_B:W_C], merged.at[W_C:W_D]
    w_d, w_e = merged.at[W_D:W_E], merged.at[W_E:W_P]
    lanes = lane_row()

    def row(k, s):
        return geo[k, pl.ds(s, 1), :]

    dv_acc[...] = jnp.zeros_like(dv_acc)
    col_w = jnp.broadcast_to(out_row[...], (128, FEAT)).T
    col_w = jnp.concatenate([col_w, col_w], axis=1)

    def middle_a(s, i):
        vec_in = v_acc[0] * row(0, s)
        for k in range(1, 3):
            vec_in += v_acc[k] * row(k, s)
        ten_in = v_acc[3] * row(3, s)
        for k in range(4, 9):
            ten_in += v_acc[k] * row(k, s)
        inner = jnp.concatenate([vec_in, ten_in], axis=0)
        back[s] = inner
        step_a[i] = mix0[s] + dot(w_b[...], stacked(tens[s] * inner))

    def middle_b(s, i):
        mixture = step_a[i]
        sg = sigmoid(mixture)
        silu = mixture * sg
        m_row[pl.ds(s, 1), :] = jnp.sum(col_w * silu, axis=0, keepdims=True)
        grad = (sg + silu * (1.0 - sg)) * row(ENV, s)
        step_b[i, : 2 * FEAT] = dot(w_c[...], stacked(grad))

    def middle_c(s, i):
        resid[s] = step_b[i, :FEAT] + col_w
        dvt = step_b[i, FEAT : 2 * FEAT]
        back[s] = dvt * back[s]
        p = dvt * tens[s]
        prod[s] = p
        step_c[i] = p

    def middle_sum(first, group):
        for k in range(9):
            part = slice(0, 32) if k < 3 else slice(32, 64)
            total = dv_acc[k]
            for i in range(group):
                total += step_c[i, part] * row(k, first + i)
            dv_acc[k] = total

    pipeline((middle_a, middle_b, middle_c), plan[1], middle_sum)

    for k in range(9):
        dv_acc[k] = env_norm * fold_sides(dv_acc[k])

    def backward_a(s, i):
        t = tens[s]
        p = prod[s]
        dt = back[s]
        vec_part, ten_part = dt[:32], dt[32:]
        for k in range(9):
            half = slice(0, 32) if k < 3 else slice(32, 64)
            moved = dv_acc[k]
            if k < 3:
                vec_part += moved * row(k, s)
            else:
                ten_part += moved * row(k, s)
            du_row[k, pl.ds(s, 1), :] = jnp.sum(
                p[half] * v_acc[k] + t[half] * moved, axis=0, keepdims=True
            )
        step_a[i] = resid[s] + dot(
            w_d[...], stacked(jnp.concatenate([vec_part, ten_part], axis=0))
        )

    def backward_b(s, i):
        dl = step_a[i]
        d_row[pl.ds(s, 1), :] = jnp.sum(dl * act[s], axis=0, keepdims=True)
        step_b[i, :16] = dot(w_e[...], stacked(dl * slope[s]))

    def backward_c(s, i):
        x, waves = basis(row(DIST, s))
        dr_row[pl.ds(s, 1), :] = jnp.sum(step_b[i, :8] * waves * x, axis=0, keepdims=True)

    pipeline((backward_a, backward_b, backward_c), plan[2])

    env, m_sum = geo[ENV], m_row[...]
    values = jnp.sum(e_row[...] + env * m_sum, axis=0, keepdims=True)
    energy[...] = jnp.broadcast_to(fold_sides(values), energy.shape)
    u = [geo[U + d] for d in range(3)]
    du = [du_row[d] for d in range(3)]
    dq = [du_row[3 + k] for k in range(6)]
    cross = ((0, 1, 3), (0, 2, 4), (1, 2, 5))
    du = [du[d] + 2.0 * u[d] * dq[d] for d in range(3)]
    for a, b, k in cross:
        du[a] = du[a] + root2 * u[b] * dq[k]
        du[b] = du[b] + root2 * u[a] * dq[k]
    inv = geo[INV]
    along = du[0] * u[0] + du[1] * u[1] + du[2] * u[2]
    dr = dr_row[...] * (-2.0 / SPACING) - along * inv
    ds = 2.0 * geo[DENV] * (d_row[...] + m_sum) + dr * inv
    zero = jnp.zeros((HALF, WIDE), f32)
    for d in range(3):
        g = du[d] * inv + geo[VEC + d] * ds
        hi, lo = halves(g)
        g_row[:, d, :] = hi.astype(f32)
        g_row[:, 3 + d, :] = lo.astype(f32)
        own = fold_sides(jnp.sum(g, axis=0, keepdims=True))
        own_sum[d : d + 1, :] = own
    g_row[:, 6, :] = zero
    g_row[:, 7, :] = zero

    s_acc[...] = jnp.zeros_like(s_acc)
    places = lax.broadcasted_iota(jnp.int32, (128, 128), 0)

    @pl.loop(0, HALF // 4, unroll=3)
    def scatter(q):
        for y in range(2):
            side = slice(128 * y, 128 * y + 128)
            left, right = [], []
            for i in range(4):
                s = 4 * q + i
                lane = lane_i[pl.ds(s, 1), :][:, side]
                col = jnp.broadcast_to(col_i[pl.ds(s, 1), :][:, side], (8, 128))
                tile = g_row[s, :, side]
                left.append(
                    jnp.concatenate(
                        [jnp.where(col == c, tile, 0.0) for c in range(9)], axis=0
                    ).astype(bf16)
                )
                right.append((places == lane).astype(f32).astype(bf16))
            s_acc[y] += lax.dot_general(
                jnp.concatenate(left, axis=1),
                jnp.concatenate(right, axis=1),
                (((1,), (1,)), ((), ())),
                preferred_element_type=f32,
            )

    if added is None:
        out[...] = jnp.zeros_like(out)
    else:
        out[0:2] = added[1:3]
        out[2:3] = jnp.zeros_like(out[2:3])
    for y in range(2):
        for c in range(9):
            tile = s_acc[y, 8 * c : 8 * c + 8, :]
            for d in range(3):
                out[c // 3, d, y + c % 3 : y + c % 3 + 1, :] += tile[d : d + 1] + tile[3 + d : 4 + d]
        own = pltpu.roll(own_sum[:, 128 * y : 128 * y + 128], 32, 1)
        kept = jnp.where((lanes >= 32) & (lanes < 96), own, 0.0)
        for d in range(3):
            out[1, d, 1 + y : 2 + y, :] -= kept[d : d + 1]


def whole(which, *refs):
    (own, sides), given, out_row, out, rest = refs[:2], refs[2:9], refs[9], refs[10:12], refs[12:]
    kept, tables, steps, rest = rest[:7], rest[7:9], rest[9:12], rest[12:]
    ghost = (own.at[0], sides.at[0], own.at[1], sides.at[1])
    front(TOGETHER, which, *ghost, *given[:1], *given[1:], *kept, *tables, *steps[:2])
    rear(TOGETHER, which, given[1], out_row, *given[5:7], None, *kept, *out, *steps, *rest)


def opening(which, ghost, ghost_z, *refs):
    blocks = (ghost.at[0], ghost.at[1], ghost_z.at[0], ghost_z.at[1])
    front(ALONE, which, *blocks, *refs)


BIG = (HALF, FEAT, WIDE)
FLAT = (HALF, WIDE)
SUMS = (9, 32, WIDE)
KEPT = (
    (BIG, f32),
    (BIG, f32),
    (BIG, f32),
    (BIG, f32),
    (SUMS, f32),
    (FLAT, f32),
    ((GEO, HALF, WIDE), f32),
)
STEPS = tuple(((STEP, rows, WIDE), f32) for rows in (FEAT, 2 * FEAT + 16, FEAT))
TABLE = (((2 * FEAT, 4 * 128), bf16), ((4, ROWS, 128), f32))
EARLY = (
    ((W_END, 3 * FEAT), bf16),
    ((8, ROWS, 128), f32),
    ((8, FEAT, 128), f32),
    ((2, FEAT, WIDE), f32),
    ((2,) + FLAT, jnp.int32),
    ((2,) + FLAT, jnp.int32),
)
REAR = (BIG, BIG, BIG, FLAT, FLAT, SUMS[:1] + FLAT, FLAT, SUMS)
REAR = REAR + ((HALF, 8, WIDE), (2, 72, 128), (8, WIDE))
REAR = tuple((shape, f32) for shape in REAR)
RESULT = (
    jax.ShapeDtypeStruct((3, 3, 4, 128), f32),
    jax.ShapeDtypeStruct((8, WIDE), f32),
)


def in_vmem(shapes):
    return [pltpu.VMEM(shape, dtype) for shape, dtype in shapes]


def call(kernel, out_shape, scratch, micros, mib):
    return pl.pallas_call(
        kernel,
        out_shape=out_shape,
        scratch_shapes=scratch,
        compiler_params=pltpu.CompilerParams(vmem_limit_bytes=mib * 2**20),
        cost_estimate=pl.CostEstimate(
            flops=micros * 1_000_000_000, bytes_accessed=2_000_000, transcendentals=2_000_000
        ),
    )


def shaped(shapes):
    return [jax.ShapeDtypeStruct(shape, dtype) for shape, dtype in shapes]


def run_early(*given):
    return call(early, shaped(EARLY), [], 2, 16)(*given)


def run_front(which, *given):
    scratch = in_vmem(TABLE + STEPS[:2])
    return call(functools.partial(opening, which), shaped(KEPT), scratch, 5, 16)(*given)


def run_rear(which, *given):
    return call(functools.partial(rear, ALONE, which), RESULT, in_vmem(STEPS + REAR), 20, 24)(*given)


def run_whole(which, *given):
    scratch = in_vmem(KEPT + TABLE + STEPS + REAR)
    return call(functools.partial(whole, which), RESULT, scratch, 12, 28)(*given)


def exchange(low, high, axis, dim):
    size = lax.axis_size(axis)
    up = [(i, (i + 1) % size) for i in range(size)]
    down = [(j, i) for i, j in up]
    if size == 2:
        return lax.ppermute(jnp.concatenate([high, low], axis=dim), axis, up)
    parts = [lax.ppermute(high, axis, up), lax.ppermute(low, axis, down)]
    return jnp.concatenate(parts, axis=dim)


def neighbours(x, axis, width):
    size = lax.axis_size(axis)
    up = [(i, (i + 1) % size) for i in range(size)]
    if size == 2:
        return lax.ppermute(x, axis, up)
    below = lax.ppermute(x, axis, up)
    above = lax.ppermute(x, axis, [(j, i) for i, j in up])
    lane = jnp.arange(x.shape[-1], dtype=jnp.int32)
    return jnp.where(lane % (2 * width) < width, above, below)


def local(
    positions,
    features,
    nbr_index,
    nbr_count,
    bin_counts,
    w_self,
    w_pair,
    w_radial,
    w_tensor,
    w_mix,
    w_out,
):
    cells_x, cells_y = nbr_count.shape[:2]
    cells_z = nbr_count.shape[2] // SLOTS
    lanes = cells_z * SLOTS
    x_index = lax.axis_index("gx")
    y_index = lax.axis_index("gy")
    z_index = lax.axis_index("gz")
    odd = x_index % 2 == 1

    def mirrored(x):
        return jnp.where(odd, x[::-1], x)

    fill = jnp.zeros((ROWS - FEAT - 3,) + positions.shape[1:], f32)
    state = jnp.concatenate([features, positions, fill], axis=0).transpose(1, 0, 2, 3)
    state = mirrored(state.reshape(cells_x, ROWS, cells_y * lanes))
    state_z = neighbours(state, "gz", SLOTS)
    size = lax.axis_size("gx")
    first = [(i, i + 1 - 2 * (i % 2)) for i in range(size)]
    second = [(i, (i - 1 + 2 * (i % 2)) % size) for i in range(size)]
    sides = neighbours(state, "gy", lanes)
    outer = lax.ppermute(state[0], "gx", second)
    inner = lax.ppermute(jnp.stack([state[1], sides[1]]), "gx", first)
    sides_z = neighbours(sides, "gz", SLOTS)
    sides_z, nbr_index, nbr_count, bin_counts = lax.optimization_barrier(
        (sides_z, nbr_index, nbr_count, bin_counts)
    )
    own_counts = lax.dynamic_slice(
        bin_counts,
        (x_index * cells_x, y_index * cells_y, z_index * cells_z),
        (cells_x, cells_y, cells_z),
    )
    slot = jnp.arange(lanes, dtype=jnp.int32) % SLOTS
    limit = jnp.where(slot < jnp.repeat(own_counts, SLOTS, axis=2), nbr_count, 0)
    limit = mirrored(limit) + MIRRORED * odd.astype(jnp.int32)
    limit = jnp.broadcast_to(limit[:, :, None, :], (cells_x, cells_y, 2, lanes))
    limit = limit.reshape(cells_x, 1, WIDE)
    codes = nbr_index.reshape(2, HALF, cells_x, cells_y, lanes)
    codes = mirrored(codes.transpose(2, 1, 3, 0, 4).reshape(cells_x, HALF, WIDE))
    inner_z = neighbours(inner, "gz", SLOTS)
    out_row = w_out[None]
    weights = (w_self, w_pair, w_radial, w_tensor, w_mix.T, out_row)
    merged, *decoded = run_early(state, sides, state_z, sides_z, codes, limit, *weights)
    outer, codes, limit = lax.optimization_barrier((outer, codes, limit))
    outer_own = jnp.stack([outer, neighbours(outer, "gz", SLOTS)])
    outer_sides = neighbours(outer_own, "gy", lanes)

    kept = run_front(1, inner, inner_z, limit, merged, *decoded)
    late_limit, kept = lax.optimization_barrier((limit, kept))
    grad0, energy0 = run_whole(0, outer_own, outer_sides, late_limit, merged, *decoded, out_row)
    back0 = lax.ppermute(grad0[0], "gx", second)
    grad1, energy1 = run_rear(1, merged, out_row, *decoded[3:], grad0, *kept)
    grad1, back0 = lax.optimization_barrier((grad1, back0))
    back1 = lax.ppermute(grad1[2], "gx", first)
    grad = grad1[:2] + jnp.stack([back0, back1])
    grad = grad[:, :, 1:-1] + exchange(grad[:, :, :1], grad[:, :, -1:], "gy", 2)
    grad = grad[..., SLOTS:-SLOTS] + exchange(grad[..., :SLOTS], grad[..., -SLOTS:], "gz", 3)
    forces = -mirrored(grad).transpose(1, 0, 2, 3)
    energies = mirrored(jnp.stack([energy0[0], energy1[0]]))
    energies = energies.reshape(cells_x, cells_y, 2, lanes)[:, :, 0]
    return forces, energies


def solution(mesh):
    return jax.shard_map(
        local,
        mesh=mesh,
        in_specs=(
            P(None, ("rep", "gx"), "gy", "gz"),
            P(None, ("rep", "gx"), "gy", "gz"),
            P(None, ("rep", "gx"), "gy", "gz"),
            P(("rep", "gx"), "gy", "gz"),
            P("rep", None, None),
            P(),
            P(),
            P(),
            P(),
            P(),
            P(),
        ),
        out_specs=(P(None, ("rep", "gx"), "gy", "gz"), P(("rep", "gx"), "gy", "gz")),
        check_vma=False,
    )
```

```python
import functools

import jax
import jax.numpy as jnp
from jax import lax
from jax.experimental import pallas as pl
from jax.experimental.pallas import tpu as pltpu
from jax.sharding import PartitionSpec as P

SLOTS = 32
cell_side = 6.0
cutoff = 6.0
soften = 0.25
env_norm = 0.25
root2 = 2.0**0.5
f32 = jnp.float32
bf16 = jnp.bfloat16
HALF = 24
WIDE = 256
FEAT = 64
ROWS = 72
BASIS = 8
MIRRORED = 64
SPACING = cutoff / (BASIS - 1)
STEP = 8
ALONE = ((8, 1), (8, 1), (8, 1))
TOGETHER = ((3, 3), (3, 3), (8, 1))

U, Q, ENV, DIST, INV, VEC, DENV, GEO = 0, 3, 9, 10, 11, 12, 15, 16


def halves(x):
    hi = x.astype(bf16)
    return hi, (x - hi.astype(f32)).astype(bf16)


def stacked(x):
    hi, lo = halves(x)
    return jnp.concatenate([hi, lo, hi], axis=0)


def stacked_left(w):
    hi, lo = halves(w)
    return jnp.concatenate([hi, hi, lo], axis=1)


def dot(a, b):
    return jnp.dot(a, b, preferred_element_type=f32)


def small_stack(x):
    hi, lo = halves(x)
    hi, lo = hi.astype(f32), lo.astype(f32)
    return jnp.concatenate([hi, lo, hi, jnp.zeros_like(hi)], axis=0)


def sigmoid(x):
    return 0.5 + 0.5 * jnp.tanh(0.5 * x)


W_A, W_B, W_C, W_D, W_E, W_P, W_S, W_R, W_END = 0, 144, 208, 336, 400, 416, 480, 544, 608


def pipeline(stages, plan, last=None):
    group, unroll = plan
    groups, depth = HALF // group, len(stages)

    def step(t, first, stop):
        for k in range(stop - 1, first - 1, -1):
            start = (t - k) * group
            for i in range(group):
                stages[k](start + i, i)
            if k == depth - 1 and last is not None:
                last(start, group)

    for t in range(depth - 1):
        step(t, 0, t + 1)
    pl.loop(depth - 1, groups, unroll=unroll)(lambda t: step(t, 0, depth))
    for t in range(groups, groups + depth - 1):
        step(t, t - groups + 1, depth)


def one_hot(index, size):
    rows = lax.broadcasted_iota(jnp.int16, (size, index.shape[1]), 0)
    return jnp.where(rows == index.astype(jnp.int16), jnp.ones((), bf16), jnp.zeros((), bf16))


def basis(dist):
    level = lax.broadcasted_iota(jnp.int32, (BASIS, 1), 0).astype(f32)
    x = dist / SPACING - level
    return x, jnp.exp(-x * x)


def lane_row():
    return lax.broadcasted_iota(jnp.int32, (1, 128), 1)


def fold_sides(x):
    return jnp.concatenate(
        [x[:, c : c + 128] + pltpu.roll(x[:, c : c + 128], 64, 1) for c in (0, 128)], axis=1
    )


def prepare(w_self, w_pair, w_radial, w_tensor, mix_t, w_out, merged):
    tensor, mix, out_row = w_tensor[...], mix_t[...].T, w_out[...]
    parts = (
        jnp.concatenate(
            [tensor.T, mix_t[:, :FEAT], jnp.broadcast_to(out_row, (16, FEAT))], axis=0
        ),
        mix_t[:, FEAT:],
        mix * out_row,
        tensor,
        jnp.concatenate([w_radial[...], jnp.zeros_like(w_radial)], axis=0),
        w_pair[...].T,
        w_self[...].T,
    )
    for first, part in zip((W_A, W_B, W_C, W_D, W_E, W_P, W_S), parts):
        merged[first : first + part.shape[0], :] = stacked_left(part)
    hi, lo = halves(w_radial[...])
    hi, lo = hi.astype(f32), lo.astype(f32)
    rows = jnp.concatenate([hi, hi, lo, jnp.zeros((168, FEAT), f32)], axis=0)
    merged[W_R:W_END, :] = rows.T.astype(bf16)


def joined_column(yc, own, sides, own_z, sides_z):
    mine, theirs = (sides, sides_z) if yc in (0, 3) else (own, own_z)
    first, second = (96, 32) if yc in (0, 2) else (32, 96)
    lanes = lane_row()
    inside = (lanes >= 32) & (lanes < 96)
    return jnp.where(inside, pltpu.roll(mine[...], first, 1), pltpu.roll(theirs[...], second, 1))


def both(x):
    return jnp.where(lane_row() < 64, pltpu.roll(x, 96, 1), pltpu.roll(x, 32, 1))


def early(
    own,
    sides,
    own_z,
    sides_z,
    codes,
    limits,
    w_self,
    w_pair,
    w_radial,
    w_tensor,
    mix_t,
    w_out,
    merged,
    columns,
    pair,
    self_t,
    lane_i,
    col_i,
):
    prepare(w_self, w_pair, w_radial, w_tensor, mix_t, w_out, merged)
    for x in range(2):
        blocks = [block.at[x] for block in (own, sides, own_z, sides_z)]
        for yc in range(4):
            columns[4 * x + yc] = joined_column(yc, *blocks)
        rows = jnp.concatenate([columns[4 * x + yc, :FEAT, :] for yc in range(4)], axis=1)
        terms = dot(merged[W_P:W_S, :], stacked(rows))
        self_terms = dot(merged[W_S:W_R, :], stacked(rows[:, 128:384]))
        for yc in range(4):
            pair[4 * x + yc] = terms[:, 128 * yc : 128 * yc + 128]
        for y in range(2):
            self_t[x, :, 128 * y : 128 * y + 128] = both(self_terms[:, 128 * y : 128 * y + 128])
        code = codes[x]
        offset = code >> 5
        plane = (offset * 43) >> 7
        dz = offset - 3 * plane
        dx = (offset * 57) >> 9
        lane256 = lax.broadcasted_iota(jnp.int32, (HALF, WIDE), 1)
        lane_i[x] = ((((lane256 >> 5) & 1) + dz) << 5) + (code & 31)
        col_i[x] = plane + jnp.where(limits[x] >= MIRRORED, 6 - 6 * dx, 0)


def front(
    plan,
    which,
    ghost_own,
    ghost_sides,
    ghost_own_z,
    ghost_sides_z,
    limit,
    merged,
    columns,
    pair,
    self_t,
    lane_i,
    col_i,
    act,
    slope,
    tens,
    mix0,
    v_acc,
    e_row,
    geo,
    table,
    ghost,
    step_a,
    step_b,
):
    w_a, w_p = merged.at[W_A:W_B], merged.at[W_P:W_S]
    w_r = merged.at[W_R:W_END, 0 : 4 * BASIS]
    self_t, lane_i, col_i = self_t.at[which], lane_i.at[which], col_i.at[which]
    far_layer = 0 if which == 0 else 2
    near_first = 3 if which == 0 else 0

    def source(dx, yc):
        return ghost.at[yc] if dx == far_layer else columns.at[4 * (dx - 1 + which) + yc]

    for yc in range(4):
        ghost[yc] = joined_column(yc, ghost_own, ghost_sides, ghost_own_z, ghost_sides_z)

    rows = jnp.concatenate([source(far_layer, yc)[:FEAT, :] for yc in range(4)], axis=1)
    hi, lo = halves(dot(w_p[...], stacked(rows)))
    table[:FEAT] = hi
    table[FEAT:] = lo

    lane256 = lax.broadcasted_iota(jnp.int32, (HALF, WIDE), 1)
    column = col_i[...]
    mirrored = (column * 11) >> 5
    limits = limit[which]
    dx = jnp.where(limits >= MIRRORED, 2 - mirrored, mirrored)
    dy = column - 3 * mirrored
    dz = (lane_i[...] >> 5) - ((lane256 >> 5) & 1)
    rank = lax.broadcasted_iota(jnp.int32, (HALF, WIDE), 0) + HALF * ((lane256 >> 6) & 1)
    mask = (rank < (limits & (MIRRORED - 1))).astype(f32)

    steps = (dx, dy, dz)
    vec = []
    for d in range(3):
        found = []
        for y in range(2):
            own = both(source(1, 1 + y)[FEAT + d : FEAT + d + 1, :])
            parts = []
            for j in range(HALF // 8):
                where = (slice(8 * j, 8 * j + 8), slice(128 * y, 128 * y + 128))
                lane, col = lane_i[where], col_i[where]
                acc = None
                for c in range(9):
                    row = source(c // 3, y + c % 3)[FEAT + d : FEAT + d + 1, :]
                    value = jnp.take_along_axis(
                        jnp.broadcast_to(row, (8, 128)), lane, axis=1, mode="promise_in_bounds"
                    )
                    acc = value if c == 0 else jnp.where(col == c, value, acc)
                parts.append(acc)
            found.append(jnp.concatenate(parts, axis=0) - own)
        vec.append(
            jnp.concatenate(found, axis=1) + cell_side * (steps[d] - 1).astype(f32)
        )
    squared = vec[0] * vec[0] + vec[1] * vec[1] + vec[2] * vec[2] + soften
    dist = jnp.sqrt(squared)
    inv = 1.0 / dist
    u = [v * inv for v in vec]
    taper = jnp.maximum(1.0 - squared / (cutoff * cutoff), 0.0)
    for d in range(3):
        geo[U + d] = u[d]
        geo[VEC + d] = vec[d]
        geo[Q + d] = u[d] * u[d] - 1.0 / 3.0
    geo[Q + 3] = root2 * u[0] * u[1]
    geo[Q + 4] = root2 * u[0] * u[2]
    geo[Q + 5] = root2 * u[1] * u[2]
    geo[ENV] = taper * taper * mask
    geo[DENV] = taper * mask * (-2.0 / (cutoff * cutoff))
    geo[DIST] = dist
    geo[INV] = inv

    def row(k, s):
        return geo[k, pl.ds(s, 1), :]

    v_acc[...] = jnp.zeros_like(v_acc)

    def gathered(s):
        lane_s = lane_i[pl.ds(s, 1), :]
        col_s = col_i[pl.ds(s, 1), :]
        far_col = col_s - 3 * far_layer + (lax.broadcasted_iota(jnp.int32, (1, WIDE), 1) >> 7)
        is_far = (col_s < 3) if which == 0 else (col_s >= 6)
        spots = jnp.where(is_far, (far_col << 7) + lane_s, -1)
        sides = []
        for y in range(2):
            lane = jnp.broadcast_to(lane_s[:, 128 * y : 128 * y + 128], (8, 128))
            col = jnp.broadcast_to(col_s[:, 128 * y : 128 * y + 128], (8, 128))
            masks = [col == c + near_first for c in range(6)]
            near = (col >= 3) if which == 0 else (col < 6)
            groups = []
            for g in range(FEAT // 8):
                acc = None
                for c in range(6):
                    value = jnp.take_along_axis(
                        pair[(c // 3) * 4 + y + c % 3, 8 * g : 8 * g + 8, :],
                        lane,
                        axis=1,
                        mode="promise_in_bounds",
                    )
                    acc = value if c == 0 else jnp.where(masks[c], value, acc)
                groups.append(jnp.where(near, acc, 0.0))
            sides.append(jnp.concatenate(groups, axis=0))
        far = dot(table[...], one_hot(spots, 512))
        return jnp.concatenate(sides, axis=1) + (far[:FEAT] + far[FEAT:])

    def forward_a(s, i):
        _, waves = basis(row(DIST, s))
        step_a[i] = dot(w_r[...], small_stack(waves).astype(bf16)) + (self_t[...] + gathered(s))

    def forward_b(s, i):
        z = step_a[i]
        sg = sigmoid(z)
        silu = z * sg
        env = row(ENV, s)
        act[s] = silu
        slope[s] = (sg + silu * (1.0 - sg)) * env
        step_b[i] = dot(w_a[...], stacked(silu * env))

    def forward_c(s, i):
        both_t = step_b[i]
        tens[s] = both_t[:FEAT]
        mix0[s] = both_t[FEAT : 2 * FEAT]
        e_row[pl.ds(s, 1), :] = both_t[2 * FEAT : 2 * FEAT + 1]

    def forward_sum(first, group):
        for k in range(9):
            part = slice(0, 32) if k < 3 else slice(32, 64)
            total = v_acc[k]
            for i in range(group):
                total += step_b[i, part] * row(k, first + i)
            v_acc[k] = total

    pipeline((forward_a, forward_b, forward_c), plan[0], forward_sum)

    for k in range(9):
        v_acc[k] = env_norm * fold_sides(v_acc[k])


def rear(
    plan,
    which,
    merged,
    out_row,
    lane_i,
    col_i,
    added,
    act,
    slope,
    tens,
    mix0,
    v_acc,
    e_row,
    geo,
    out,
    energy,
    step_a,
    step_b,
    step_c,
    prod,
    back,
    resid,
    m_row,
    d_row,
    du_row,
    dr_row,
    dv_acc,
    g_row,
    s_acc,
    own_sum,
):
    lane_i, col_i = lane_i.at[which], col_i.at[which]
    w_b, w_c = merged.at[W_B:W_C], merged.at[W_C:W_D]
    w_d, w_e = merged.at[W_D:W_E], merged.at[W_E:W_P]
    lanes = lane_row()

    def row(k, s):
        return geo[k, pl.ds(s, 1), :]

    dv_acc[...] = jnp.zeros_like(dv_acc)
    col_w = jnp.broadcast_to(out_row[...], (128, FEAT)).T
    col_w = jnp.concatenate([col_w, col_w], axis=1)

    def middle_a(s, i):
        vec_in = v_acc[0] * row(0, s)
        for k in range(1, 3):
            vec_in += v_acc[k] * row(k, s)
        ten_in = v_acc[3] * row(3, s)
        for k in range(4, 9):
            ten_in += v_acc[k] * row(k, s)
        inner = jnp.concatenate([vec_in, ten_in], axis=0)
        back[s] = inner
        step_a[i] = mix0[s] + dot(w_b[...], stacked(tens[s] * inner))

    def middle_b(s, i):
        mixture = step_a[i]
        sg = sigmoid(mixture)
        silu = mixture * sg
        m_row[pl.ds(s, 1), :] = jnp.sum(col_w * silu, axis=0, keepdims=True)
        grad = (sg + silu * (1.0 - sg)) * row(ENV, s)
        step_b[i, : 2 * FEAT] = dot(w_c[...], stacked(grad))

    def middle_c(s, i):
        resid[s] = step_b[i, :FEAT] + col_w
        dvt = step_b[i, FEAT : 2 * FEAT]
        back[s] = dvt * back[s]
        p = dvt * tens[s]
        prod[s] = p
        step_c[i] = p

    def middle_sum(first, group):
        for k in range(9):
            part = slice(0, 32) if k < 3 else slice(32, 64)
            total = dv_acc[k]
            for i in range(group):
                total += step_c[i, part] * row(k, first + i)
            dv_acc[k] = total

    pipeline((middle_a, middle_b, middle_c), plan[1], middle_sum)

    for k in range(9):
        dv_acc[k] = env_norm * fold_sides(dv_acc[k])

    def backward_a(s, i):
        t = tens[s]
        p = prod[s]
        dt = back[s]
        vec_part, ten_part = dt[:32], dt[32:]
        for k in range(9):
            half = slice(0, 32) if k < 3 else slice(32, 64)
            moved = dv_acc[k]
            if k < 3:
                vec_part += moved * row(k, s)
            else:
                ten_part += moved * row(k, s)
            du_row[k, pl.ds(s, 1), :] = jnp.sum(
                p[half] * v_acc[k] + t[half] * moved, axis=0, keepdims=True
            )
        step_a[i] = resid[s] + dot(
            w_d[...], stacked(jnp.concatenate([vec_part, ten_part], axis=0))
        )

    def backward_b(s, i):
        dl = step_a[i]
        d_row[pl.ds(s, 1), :] = jnp.sum(dl * act[s], axis=0, keepdims=True)
        step_b[i, :16] = dot(w_e[...], stacked(dl * slope[s]))

    def backward_c(s, i):
        x, waves = basis(row(DIST, s))
        dr_row[pl.ds(s, 1), :] = jnp.sum(step_b[i, :8] * waves * x, axis=0, keepdims=True)

    pipeline((backward_a, backward_b, backward_c), plan[2])

    env, m_sum = geo[ENV], m_row[...]
    values = jnp.sum(e_row[...] + env * m_sum, axis=0, keepdims=True)
    energy[...] = jnp.broadcast_to(fold_sides(values), energy.shape)
    u = [geo[U + d] for d in range(3)]
    du = [du_row[d] for d in range(3)]
    dq = [du_row[3 + k] for k in range(6)]
    cross = ((0, 1, 3), (0, 2, 4), (1, 2, 5))
    du = [du[d] + 2.0 * u[d] * dq[d] for d in range(3)]
    for a, b, k in cross:
        du[a] = du[a] + root2 * u[b] * dq[k]
        du[b] = du[b] + root2 * u[a] * dq[k]
    inv = geo[INV]
    along = du[0] * u[0] + du[1] * u[1] + du[2] * u[2]
    dr = dr_row[...] * (-2.0 / SPACING) - along * inv
    ds = 2.0 * geo[DENV] * (d_row[...] + m_sum) + dr * inv
    zero = jnp.zeros((HALF, WIDE), f32)
    for d in range(3):
        g = du[d] * inv + geo[VEC + d] * ds
        hi, lo = halves(g)
        g_row[:, d, :] = hi.astype(f32)
        g_row[:, 3 + d, :] = lo.astype(f32)
        own = fold_sides(jnp.sum(g, axis=0, keepdims=True))
        own_sum[d : d + 1, :] = own
    g_row[:, 6, :] = zero
    g_row[:, 7, :] = zero

    s_acc[...] = jnp.zeros_like(s_acc)

    @pl.loop(0, HALF // 4, unroll=6)
    def scatter(q):
        for y in range(2):
            side = slice(128 * y, 128 * y + 128)
            left, right = [], []
            for i in range(4):
                s = 4 * q + i
                lane = lane_i[pl.ds(s, 1), :][:, side]
                col = jnp.broadcast_to(col_i[pl.ds(s, 1), :][:, side], (8, 128))
                tile = g_row[s, :, side]
                left.append(
                    jnp.concatenate(
                        [jnp.where(col == c, tile, 0.0) for c in range(9)], axis=0
                    ).astype(bf16)
                )
                right.append(one_hot(lane, 128))
            s_acc[y] += lax.dot_general(
                jnp.concatenate(left, axis=1),
                jnp.concatenate(right, axis=1),
                (((1,), (1,)), ((), ())),
                preferred_element_type=f32,
            )

    if added is None:
        out[...] = jnp.zeros_like(out)
    else:
        out[0:2] = added[1:3]
        out[2:3] = jnp.zeros_like(out[2:3])
    for y in range(2):
        for c in range(9):
            tile = s_acc[y, 8 * c : 8 * c + 8, :]
            for d in range(3):
                out[c // 3, d, y + c % 3 : y + c % 3 + 1, :] += tile[d : d + 1] + tile[3 + d : 4 + d]
        own = pltpu.roll(own_sum[:, 128 * y : 128 * y + 128], 32, 1)
        kept = jnp.where((lanes >= 32) & (lanes < 96), own, 0.0)
        for d in range(3):
            out[1, d, 1 + y : 2 + y, :] -= kept[d : d + 1]


def whole(which, *refs):
    (own, sides), given, out_row, out, rest = refs[:2], refs[2:9], refs[9], refs[10:12], refs[12:]
    kept, tables, steps, rest = rest[:7], rest[7:9], rest[9:12], rest[12:]
    ghost = (own.at[0], sides.at[0], own.at[1], sides.at[1])
    front(TOGETHER, which, *ghost, *given[:1], *given[1:], *kept, *tables, *steps[:2])
    rear(TOGETHER, which, given[1], out_row, *given[5:7], None, *kept, *out, *steps, *rest)


def opening(which, ghost, ghost_z, *refs):
    blocks = (ghost.at[0], ghost.at[1], ghost_z.at[0], ghost_z.at[1])
    front(ALONE, which, *blocks, *refs)


BIG = (HALF, FEAT, WIDE)
FLAT = (HALF, WIDE)
SUMS = (9, 32, WIDE)
KEPT = (
    (BIG, f32),
    (BIG, f32),
    (BIG, f32),
    (BIG, f32),
    (SUMS, f32),
    (FLAT, f32),
    ((GEO, HALF, WIDE), f32),
)
STEPS = tuple(((STEP, rows, WIDE), f32) for rows in (FEAT, 2 * FEAT + 16, FEAT))
TABLE = (((2 * FEAT, 4 * 128), bf16), ((4, ROWS, 128), f32))
EARLY = (
    ((W_END, 3 * FEAT), bf16),
    ((8, ROWS, 128), f32),
    ((8, FEAT, 128), f32),
    ((2, FEAT, WIDE), f32),
    ((2,) + FLAT, jnp.int32),
    ((2,) + FLAT, jnp.int32),
)
REAR = (BIG, BIG, BIG, FLAT, FLAT, SUMS[:1] + FLAT, FLAT, SUMS)
REAR = REAR + ((HALF, 8, WIDE), (2, 72, 128), (8, WIDE))
REAR = tuple((shape, f32) for shape in REAR)
RESULT = (
    jax.ShapeDtypeStruct((3, 3, 4, 128), f32),
    jax.ShapeDtypeStruct((8, WIDE), f32),
)


def in_vmem(shapes):
    return [pltpu.VMEM(shape, dtype) for shape, dtype in shapes]


def call(kernel, out_shape, scratch, micros, mib):
    return pl.pallas_call(
        kernel,
        out_shape=out_shape,
        scratch_shapes=scratch,
        compiler_params=pltpu.CompilerParams(vmem_limit_bytes=mib * 2**20),
        cost_estimate=pl.CostEstimate(
            flops=micros * 1_000_000_000, bytes_accessed=2_000_000, transcendentals=2_000_000
        ),
    )


def shaped(shapes):
    return [jax.ShapeDtypeStruct(shape, dtype) for shape, dtype in shapes]


def run_early(*given):
    return call(early, shaped(EARLY), [], 2, 16)(*given)


def run_front(which, *given):
    scratch = in_vmem(TABLE + STEPS[:2])
    return call(functools.partial(opening, which), shaped(KEPT), scratch, 5, 16)(*given)


def run_rear(which, *given):
    return call(functools.partial(rear, ALONE, which), RESULT, in_vmem(STEPS + REAR), 20, 24)(*given)


def run_whole(which, *given):
    scratch = in_vmem(KEPT + TABLE + STEPS + REAR)
    return call(functools.partial(whole, which), RESULT, scratch, 12, 28)(*given)


def exchange(low, high, axis, dim):
    size = lax.axis_size(axis)
    up = [(i, (i + 1) % size) for i in range(size)]
    down = [(j, i) for i, j in up]
    if size == 2:
        return lax.ppermute(jnp.concatenate([high, low], axis=dim), axis, up)
    parts = [lax.ppermute(high, axis, up), lax.ppermute(low, axis, down)]
    return jnp.concatenate(parts, axis=dim)


def neighbours(x, axis, width):
    size = lax.axis_size(axis)
    up = [(i, (i + 1) % size) for i in range(size)]
    if size == 2:
        return lax.ppermute(x, axis, up)
    below = lax.ppermute(x, axis, up)
    above = lax.ppermute(x, axis, [(j, i) for i, j in up])
    lane = jnp.arange(x.shape[-1], dtype=jnp.int32)
    return jnp.where(lane % (2 * width) < width, above, below)


def local(
    positions,
    features,
    nbr_index,
    nbr_count,
    bin_counts,
    w_self,
    w_pair,
    w_radial,
    w_tensor,
    w_mix,
    w_out,
):
    cells_x, cells_y = nbr_count.shape[:2]
    cells_z = nbr_count.shape[2] // SLOTS
    lanes = cells_z * SLOTS
    x_index = lax.axis_index("gx")
    y_index = lax.axis_index("gy")
    z_index = lax.axis_index("gz")
    odd = x_index % 2 == 1

    def mirrored(x):
        return jnp.where(odd, x[::-1], x)

    fill = jnp.zeros((ROWS - FEAT - 3,) + positions.shape[1:], f32)
    state = jnp.concatenate([features, positions, fill], axis=0).transpose(1, 0, 2, 3)
    state = mirrored(state.reshape(cells_x, ROWS, cells_y * lanes))
    state_z = neighbours(state, "gz", SLOTS)
    size = lax.axis_size("gx")
    first = [(i, i + 1 - 2 * (i % 2)) for i in range(size)]
    second = [(i, (i - 1 + 2 * (i % 2)) % size) for i in range(size)]
    sides = neighbours(state, "gy", lanes)
    outer = lax.ppermute(state[0], "gx", second)
    inner = lax.ppermute(jnp.stack([state[1], sides[1]]), "gx", first)
    sides_z = neighbours(sides, "gz", SLOTS)
    sides_z, nbr_index, nbr_count, bin_counts = lax.optimization_barrier(
        (sides_z, nbr_index, nbr_count, bin_counts)
    )
    own_counts = lax.dynamic_slice(
        bin_counts,
        (x_index * cells_x, y_index * cells_y, z_index * cells_z),
        (cells_x, cells_y, cells_z),
    )
    slot = jnp.arange(lanes, dtype=jnp.int32) % SLOTS
    limit = jnp.where(slot < jnp.repeat(own_counts, SLOTS, axis=2), nbr_count, 0)
    limit = mirrored(limit) + MIRRORED * odd.astype(jnp.int32)
    limit = jnp.broadcast_to(limit[:, :, None, :], (cells_x, cells_y, 2, lanes))
    limit = limit.reshape(cells_x, 1, WIDE)
    codes = nbr_index.reshape(2, HALF, cells_x, cells_y, lanes)
    codes = mirrored(codes.transpose(2, 1, 3, 0, 4).reshape(cells_x, HALF, WIDE))
    outer, codes, limit = lax.optimization_barrier((outer, codes, limit))
    out_row = w_out[None]
    weights = (w_self, w_pair, w_radial, w_tensor, w_mix.T, out_row)
    merged, *decoded = run_early(state, sides, state_z, sides_z, codes, limit, *weights)
    inner, merged = lax.optimization_barrier((inner, merged))
    inner_z = neighbours(inner, "gz", SLOTS)
    outer_own = jnp.stack([outer, neighbours(outer, "gz", SLOTS)])
    outer_sides = neighbours(outer_own, "gy", lanes)

    kept = run_front(1, inner, inner_z, limit, merged, *decoded)
    late_limit, kept = lax.optimization_barrier((limit, kept))
    grad0, energy0 = run_whole(0, outer_own, outer_sides, late_limit, merged, *decoded, out_row)
    back0 = lax.ppermute(grad0[0], "gx", second)
    grad1, energy1 = run_rear(1, merged, out_row, *decoded[3:], grad0, *kept)
    grad1, back0 = lax.optimization_barrier((grad1, back0))
    back1 = lax.ppermute(grad1[2], "gx", first)
    grad = grad1[:2] + jnp.stack([back0, back1])
    grad = grad[:, :, 1:-1] + exchange(grad[:, :, :1], grad[:, :, -1:], "gy", 2)
    grad = grad[..., SLOTS:-SLOTS] + exchange(grad[..., :SLOTS], grad[..., -SLOTS:], "gz", 3)
    forces = -mirrored(grad).transpose(1, 0, 2, 3)
    energies = mirrored(jnp.stack([energy0[0], energy1[0]]))
    energies = energies.reshape(cells_x, cells_y, 2, lanes)[:, :, 0]
    return forces, energies


def solution(mesh):
    return jax.shard_map(
        local,
        mesh=mesh,
        in_specs=(
            P(None, ("rep", "gx"), "gy", "gz"),
            P(None, ("rep", "gx"), "gy", "gz"),
            P(None, ("rep", "gx"), "gy", "gz"),
            P(("rep", "gx"), "gy", "gz"),
            P("rep", None, None),
            P(),
            P(),
            P(),
            P(),
            P(),
            P(),
        ),
        out_specs=(P(None, ("rep", "gx"), "gy", "gz"), P(("rep", "gx"), "gy", "gz")),
        check_vma=False,
    )
```

```python
import functools

import jax
import jax.numpy as jnp
from jax import lax
from jax.experimental import pallas as pl
from jax.experimental.pallas import tpu as pltpu
from jax.sharding import PartitionSpec as P

SLOTS = 32
cell_side = 6.0
cutoff = 6.0
soften = 0.25
env_norm = 0.25
root2 = 2.0**0.5
f32 = jnp.float32
bf16 = jnp.bfloat16
HALF = 24
WIDE = 256
FEAT = 64
ROWS = 72
BASIS = 8
MIRRORED = 64
SPACING = cutoff / (BASIS - 1)
STEP = 8
ALONE = ((8, 1), (8, 1), (8, 1))
TOGETHER = ((3, 3), (3, 3), (8, 1))

U, Q, ENV, DIST, INV, VEC, DENV, GEO = 0, 3, 9, 10, 11, 12, 15, 16


def halves(x):
    hi = x.astype(bf16)
    return hi, (x - hi.astype(f32)).astype(bf16)


def stacked(x):
    hi, lo = halves(x)
    return jnp.concatenate([hi, lo, hi], axis=0)


def stacked_left(w):
    hi, lo = halves(w)
    return jnp.concatenate([hi, hi, lo], axis=1)


def dot(a, b):
    return jnp.dot(a, b, preferred_element_type=f32)


def small_stack(x):
    hi, lo = halves(x)
    hi, lo = hi.astype(f32), lo.astype(f32)
    return jnp.concatenate([hi, lo, hi, jnp.zeros_like(hi)], axis=0)


def sigmoid(x):
    return 0.5 + 0.5 * jnp.tanh(0.5 * x)


W_A, W_B, W_C, W_D, W_E, W_P, W_S, W_R, W_END = 0, 144, 208, 336, 400, 416, 480, 544, 608


def pipeline(stages, plan, last=None):
    group, unroll = plan
    groups, depth = HALF // group, len(stages)

    def step(t, first, stop):
        for k in range(stop - 1, first - 1, -1):
            start = (t - k) * group
            for i in range(group):
                stages[k](start + i, i)
            if k == depth - 1 and last is not None:
                last(start, group)

    for t in range(depth - 1):
        step(t, 0, t + 1)
    pl.loop(depth - 1, groups, unroll=unroll)(lambda t: step(t, 0, depth))
    for t in range(groups, groups + depth - 1):
        step(t, t - groups + 1, depth)


def one_hot(index, size):
    rows = lax.broadcasted_iota(jnp.int16, (size, index.shape[1]), 0)
    return jnp.where(rows == index.astype(jnp.int16), jnp.ones((), bf16), jnp.zeros((), bf16))


def basis(dist):
    level = lax.broadcasted_iota(jnp.int32, (BASIS, 1), 0).astype(f32)
    x = dist / SPACING - level
    return x, jnp.exp(-x * x)


def lane_row():
    return lax.broadcasted_iota(jnp.int32, (1, 128), 1)


def fold_sides(x):
    return jnp.concatenate(
        [x[:, c : c + 128] + pltpu.roll(x[:, c : c + 128], 64, 1) for c in (0, 128)], axis=1
    )


def prepare(w_self, w_pair, w_radial, w_tensor, mix_t, w_out, merged):
    tensor, mix, out_row = w_tensor[...], mix_t[...].T, w_out[...]
    parts = (
        jnp.concatenate(
            [tensor.T, mix_t[:, :FEAT], jnp.broadcast_to(out_row, (16, FEAT))], axis=0
        ),
        mix_t[:, FEAT:],
        mix * out_row,
        tensor,
        jnp.concatenate([w_radial[...], jnp.zeros_like(w_radial)], axis=0),
        w_pair[...].T,
        w_self[...].T,
    )
    for first, part in zip((W_A, W_B, W_C, W_D, W_E, W_P, W_S), parts):
        merged[first : first + part.shape[0], :] = stacked_left(part)
    hi, lo = halves(w_radial[...])
    hi, lo = hi.astype(f32), lo.astype(f32)
    rows = jnp.concatenate([hi, hi, lo, jnp.zeros((168, FEAT), f32)], axis=0)
    merged[W_R:W_END, :] = rows.T.astype(bf16)


def joined_column(yc, own, sides, own_z, sides_z):
    mine, theirs = (sides, sides_z) if yc in (0, 3) else (own, own_z)
    first, second = (96, 32) if yc in (0, 2) else (32, 96)
    lanes = lane_row()
    inside = (lanes >= 32) & (lanes < 96)
    return jnp.where(inside, pltpu.roll(mine[...], first, 1), pltpu.roll(theirs[...], second, 1))


def both(x):
    return jnp.where(lane_row() < 64, pltpu.roll(x, 96, 1), pltpu.roll(x, 32, 1))


def early(
    own,
    sides,
    own_z,
    sides_z,
    codes,
    limits,
    w_self,
    w_pair,
    w_radial,
    w_tensor,
    mix_t,
    w_out,
    merged,
    columns,
    pair,
    self_t,
    lane_i,
    col_i,
):
    prepare(w_self, w_pair, w_radial, w_tensor, mix_t, w_out, merged)
    for x in range(2):
        blocks = [block.at[x] for block in (own, sides, own_z, sides_z)]
        for yc in range(4):
            columns[4 * x + yc] = joined_column(yc, *blocks)
        rows = jnp.concatenate([columns[4 * x + yc, :FEAT, :] for yc in range(4)], axis=1)
        terms = dot(merged[W_P:W_S, :], stacked(rows))
        self_terms = dot(merged[W_S:W_R, :], stacked(rows[:, 128:384]))
        for yc in range(4):
            pair[4 * x + yc] = terms[:, 128 * yc : 128 * yc + 128]
        for y in range(2):
            self_t[x, :, 128 * y : 128 * y + 128] = both(self_terms[:, 128 * y : 128 * y + 128])
        code = codes[x]
        offset = code >> 5
        plane = (offset * 43) >> 7
        dz = offset - 3 * plane
        dx = (offset * 57) >> 9
        lane256 = lax.broadcasted_iota(jnp.int32, (HALF, WIDE), 1)
        lane_i[x] = ((((lane256 >> 5) & 1) + dz) << 5) + (code & 31)
        col_i[x] = plane + jnp.where(limits[x] >= MIRRORED, 6 - 6 * dx, 0)


def front(
    plan,
    which,
    ghost_own,
    ghost_sides,
    ghost_own_z,
    ghost_sides_z,
    limit,
    merged,
    columns,
    pair,
    self_t,
    lane_i,
    col_i,
    act,
    slope,
    tens,
    mix0,
    v_acc,
    e_row,
    geo,
    table,
    ghost,
    step_a,
    step_b,
):
    w_a, w_p = merged.at[W_A:W_B], merged.at[W_P:W_S]
    w_r = merged.at[W_R:W_END, 0 : 4 * BASIS]
    self_t, lane_i, col_i = self_t.at[which], lane_i.at[which], col_i.at[which]
    far_layer = 0 if which == 0 else 2
    near_first = 3 if which == 0 else 0

    def source(dx, yc):
        return ghost.at[yc] if dx == far_layer else columns.at[4 * (dx - 1 + which) + yc]

    for yc in range(4):
        ghost[yc] = joined_column(yc, ghost_own, ghost_sides, ghost_own_z, ghost_sides_z)

    rows = jnp.concatenate([source(far_layer, yc)[:FEAT, :] for yc in range(4)], axis=1)
    hi, lo = halves(dot(w_p[...], stacked(rows)))
    table[:FEAT] = hi
    table[FEAT:] = lo

    lane256 = lax.broadcasted_iota(jnp.int32, (HALF, WIDE), 1)
    column = col_i[...]
    mirrored = (column * 11) >> 5
    limits = limit[which]
    dx = jnp.where(limits >= MIRRORED, 2 - mirrored, mirrored)
    dy = column - 3 * mirrored
    dz = (lane_i[...] >> 5) - ((lane256 >> 5) & 1)
    rank = lax.broadcasted_iota(jnp.int32, (HALF, WIDE), 0) + HALF * ((lane256 >> 6) & 1)
    mask = (rank < (limits & (MIRRORED - 1))).astype(f32)

    steps = (dx, dy, dz)
    vec = []
    for d in range(3):
        found = []
        for y in range(2):
            own = both(source(1, 1 + y)[FEAT + d : FEAT + d + 1, :])
            parts = []
            for j in range(HALF // 8):
                where = (slice(8 * j, 8 * j + 8), slice(128 * y, 128 * y + 128))
                lane, col = lane_i[where], col_i[where]
                acc = None
                for c in range(9):
                    row = source(c // 3, y + c % 3)[FEAT + d : FEAT + d + 1, :]
                    value = jnp.take_along_axis(
                        jnp.broadcast_to(row, (8, 128)), lane, axis=1, mode="promise_in_bounds"
                    )
                    acc = value if c == 0 else jnp.where(col == c, value, acc)
                parts.append(acc)
            found.append(jnp.concatenate(parts, axis=0) - own)
        vec.append(
            jnp.concatenate(found, axis=1) + cell_side * (steps[d] - 1).astype(f32)
        )
    squared = vec[0] * vec[0] + vec[1] * vec[1] + vec[2] * vec[2] + soften
    dist = jnp.sqrt(squared)
    inv = 1.0 / dist
    u = [v * inv for v in vec]
    taper = jnp.maximum(1.0 - squared / (cutoff * cutoff), 0.0)
    for d in range(3):
        geo[U + d] = u[d]
        geo[VEC + d] = vec[d]
        geo[Q + d] = u[d] * u[d] - 1.0 / 3.0
    geo[Q + 3] = root2 * u[0] * u[1]
    geo[Q + 4] = root2 * u[0] * u[2]
    geo[Q + 5] = root2 * u[1] * u[2]
    geo[ENV] = taper * taper * mask
    geo[DENV] = taper * mask * (-2.0 / (cutoff * cutoff))
    geo[DIST] = dist
    geo[INV] = inv

    def row(k, s):
        return geo[k, pl.ds(s, 1), :]

    v_acc[...] = jnp.zeros_like(v_acc)

    def gathered(s):
        lane_s = lane_i[pl.ds(s, 1), :]
        col_s = col_i[pl.ds(s, 1), :]
        far_col = col_s - 3 * far_layer + (lax.broadcasted_iota(jnp.int32, (1, WIDE), 1) >> 7)
        is_far = (col_s < 3) if which == 0 else (col_s >= 6)
        spots = jnp.where(is_far, (far_col << 7) + lane_s, -1)
        sides = []
        for y in range(2):
            lane = jnp.broadcast_to(lane_s[:, 128 * y : 128 * y + 128], (8, 128))
            col = jnp.broadcast_to(col_s[:, 128 * y : 128 * y + 128], (8, 128))
            masks = [col == c + near_first for c in range(6)]
            near = (col >= 3) if which == 0 else (col < 6)
            groups = []
            for g in range(FEAT // 8):
                acc = None
                for c in range(6):
                    value = jnp.take_along_axis(
                        pair[(c // 3) * 4 + y + c % 3, 8 * g : 8 * g + 8, :],
                        lane,
                        axis=1,
                        mode="promise_in_bounds",
                    )
                    acc = value if c == 0 else jnp.where(masks[c], value, acc)
                groups.append(jnp.where(near, acc, 0.0))
            sides.append(jnp.concatenate(groups, axis=0))
        far = dot(table[...], one_hot(spots, 512))
        return jnp.concatenate(sides, axis=1) + (far[:FEAT] + far[FEAT:])

    def forward_a(s, i):
        _, waves = basis(row(DIST, s))
        step_a[i] = dot(w_r[...], small_stack(waves).astype(bf16)) + (self_t[...] + gathered(s))

    def forward_b(s, i):
        z = step_a[i]
        sg = sigmoid(z)
        silu = z * sg
        env = row(ENV, s)
        act[s] = silu
        slope[s] = (sg + silu * (1.0 - sg)) * env
        step_b[i] = dot(w_a[...], stacked(silu * env))

    def forward_c(s, i):
        both_t = step_b[i]
        tens[s] = both_t[:FEAT]
        mix0[s] = both_t[FEAT : 2 * FEAT]
        e_row[pl.ds(s, 1), :] = both_t[2 * FEAT : 2 * FEAT + 1]

    def forward_sum(first, group):
        for k in range(9):
            part = slice(0, 32) if k < 3 else slice(32, 64)
            total = v_acc[k]
            for i in range(group):
                total += step_b[i, part] * row(k, first + i)
            v_acc[k] = total

    pipeline((forward_a, forward_b, forward_c), plan[0], forward_sum)

    for k in range(9):
        v_acc[k] = env_norm * fold_sides(v_acc[k])


def rear(
    plan,
    which,
    merged,
    out_row,
    lane_i,
    col_i,
    added,
    act,
    slope,
    tens,
    mix0,
    v_acc,
    e_row,
    geo,
    out,
    energy,
    step_a,
    step_b,
    step_c,
    prod,
    back,
    resid,
    m_row,
    d_row,
    du_row,
    dr_row,
    dv_acc,
    g_row,
    s_acc,
    own_sum,
):
    lane_i, col_i = lane_i.at[which], col_i.at[which]
    w_b, w_c = merged.at[W_B:W_C], merged.at[W_C:W_D]
    w_d, w_e = merged.at[W_D:W_E], merged.at[W_E:W_P]
    lanes = lane_row()

    def row(k, s):
        return geo[k, pl.ds(s, 1), :]

    dv_acc[...] = jnp.zeros_like(dv_acc)
    col_w = jnp.broadcast_to(out_row[...], (128, FEAT)).T
    col_w = jnp.concatenate([col_w, col_w], axis=1)

    def middle_a(s, i):
        vec_in = v_acc[0] * row(0, s)
        for k in range(1, 3):
            vec_in += v_acc[k] * row(k, s)
        ten_in = v_acc[3] * row(3, s)
        for k in range(4, 9):
            ten_in += v_acc[k] * row(k, s)
        inner = jnp.concatenate([vec_in, ten_in], axis=0)
        back[s] = inner
        step_a[i] = mix0[s] + dot(w_b[...], stacked(tens[s] * inner))

    def middle_b(s, i):
        mixture = step_a[i]
        sg = sigmoid(mixture)
        silu = mixture * sg
        m_row[pl.ds(s, 1), :] = jnp.sum(col_w * silu, axis=0, keepdims=True)
        grad = (sg + silu * (1.0 - sg)) * row(ENV, s)
        step_b[i, : 2 * FEAT] = dot(w_c[...], stacked(grad))

    def middle_c(s, i):
        resid[s] = step_b[i, :FEAT] + col_w
        dvt = step_b[i, FEAT : 2 * FEAT]
        back[s] = dvt * back[s]
        p = dvt * tens[s]
        prod[s] = p
        step_c[i] = p

    def middle_sum(first, group):
        for k in range(9):
            part = slice(0, 32) if k < 3 else slice(32, 64)
            total = dv_acc[k]
            for i in range(group):
                total += step_c[i, part] * row(k, first + i)
            dv_acc[k] = total

    pipeline((middle_a, middle_b, middle_c), plan[1], middle_sum)

    for k in range(9):
        dv_acc[k] = env_norm * fold_sides(dv_acc[k])

    def backward_a(s, i):
        t = tens[s]
        p = prod[s]
        dt = back[s]
        vec_part, ten_part = dt[:32], dt[32:]
        for k in range(9):
            half = slice(0, 32) if k < 3 else slice(32, 64)
            moved = dv_acc[k]
            if k < 3:
                vec_part += moved * row(k, s)
            else:
                ten_part += moved * row(k, s)
            du_row[k, pl.ds(s, 1), :] = jnp.sum(
                p[half] * v_acc[k] + t[half] * moved, axis=0, keepdims=True
            )
        step_a[i] = resid[s] + dot(
            w_d[...], stacked(jnp.concatenate([vec_part, ten_part], axis=0))
        )

    def backward_b(s, i):
        dl = step_a[i]
        d_row[pl.ds(s, 1), :] = jnp.sum(dl * act[s], axis=0, keepdims=True)
        step_b[i, :16] = dot(w_e[...], stacked(dl * slope[s]))

    def backward_c(s, i):
        x, waves = basis(row(DIST, s))
        dr_row[pl.ds(s, 1), :] = jnp.sum(step_b[i, :8] * waves * x, axis=0, keepdims=True)

    pipeline((backward_a, backward_b, backward_c), plan[2])

    env, m_sum = geo[ENV], m_row[...]
    values = jnp.sum(e_row[...] + env * m_sum, axis=0, keepdims=True)
    energy[...] = jnp.broadcast_to(fold_sides(values), energy.shape)
    u = [geo[U + d] for d in range(3)]
    du = [du_row[d] for d in range(3)]
    dq = [du_row[3 + k] for k in range(6)]
    cross = ((0, 1, 3), (0, 2, 4), (1, 2, 5))
    du = [du[d] + 2.0 * u[d] * dq[d] for d in range(3)]
    for a, b, k in cross:
        du[a] = du[a] + root2 * u[b] * dq[k]
        du[b] = du[b] + root2 * u[a] * dq[k]
    inv = geo[INV]
    along = du[0] * u[0] + du[1] * u[1] + du[2] * u[2]
    dr = dr_row[...] * (-2.0 / SPACING) - along * inv
    ds = 2.0 * geo[DENV] * (d_row[...] + m_sum) + dr * inv
    zero = jnp.zeros((HALF, WIDE), f32)
    for d in range(3):
        g = du[d] * inv + geo[VEC + d] * ds
        hi, lo = halves(g)
        g_row[:, d, :] = hi.astype(f32)
        g_row[:, 3 + d, :] = lo.astype(f32)
        own = fold_sides(jnp.sum(g, axis=0, keepdims=True))
        own_sum[d : d + 1, :] = own
    g_row[:, 6, :] = zero
    g_row[:, 7, :] = zero

    s_acc[...] = jnp.zeros_like(s_acc)

    @pl.loop(0, HALF // 4, unroll=6)
    def scatter(q):
        for y in range(2):
            side = slice(128 * y, 128 * y + 128)
            left, right = [], []
            for i in range(4):
                s = 4 * q + i
                lane = lane_i[pl.ds(s, 1), :][:, side]
                col = jnp.broadcast_to(col_i[pl.ds(s, 1), :][:, side], (8, 128))
                tile = g_row[s, :, side]
                left.append(
                    jnp.concatenate(
                        [jnp.where(col == c, tile, 0.0) for c in range(9)], axis=0
                    ).astype(bf16)
                )
                right.append(one_hot(lane, 128))
            s_acc[y] += lax.dot_general(
                jnp.concatenate(left, axis=1),
                jnp.concatenate(right, axis=1),
                (((1,), (1,)), ((), ())),
                preferred_element_type=f32,
            )

    if added is None:
        out[...] = jnp.zeros_like(out)
    else:
        out[0:2] = added[1:3]
        out[2:3] = jnp.zeros_like(out[2:3])
    for y in range(2):
        for c in range(9):
            tile = s_acc[y, 8 * c : 8 * c + 8, :]
            for d in range(3):
                out[c // 3, d, y + c % 3 : y + c % 3 + 1, :] += tile[d : d + 1] + tile[3 + d : 4 + d]
        own = pltpu.roll(own_sum[:, 128 * y : 128 * y + 128], 32, 1)
        kept = jnp.where((lanes >= 32) & (lanes < 96), own, 0.0)
        for d in range(3):
            out[1, d, 1 + y : 2 + y, :] -= kept[d : d + 1]


def whole(which, *refs):
    (own, sides), given, out_row, out, rest = refs[:2], refs[2:9], refs[9], refs[10:12], refs[12:]
    kept, tables, steps, rest = rest[:7], rest[7:9], rest[9:12], rest[12:]
    ghost = (own.at[0], sides.at[0], own.at[1], sides.at[1])
    front(TOGETHER, which, *ghost, *given[:1], *given[1:], *kept, *tables, *steps[:2])
    rear(TOGETHER, which, given[1], out_row, *given[5:7], None, *kept, *out, *steps, *rest)


def opening(which, ghost, ghost_z, *refs):
    blocks = (ghost.at[0], ghost.at[1], ghost_z.at[0], ghost_z.at[1])
    front(ALONE, which, *blocks, *refs)


BIG = (HALF, FEAT, WIDE)
FLAT = (HALF, WIDE)
SUMS = (9, 32, WIDE)
KEPT = (
    (BIG, f32),
    (BIG, f32),
    (BIG, f32),
    (BIG, f32),
    (SUMS, f32),
    (FLAT, f32),
    ((GEO, HALF, WIDE), f32),
)
STEPS = tuple(((STEP, rows, WIDE), f32) for rows in (FEAT, 2 * FEAT + 16, FEAT))
TABLE = (((2 * FEAT, 4 * 128), bf16), ((4, ROWS, 128), f32))
EARLY = (
    ((W_END, 3 * FEAT), bf16),
    ((8, ROWS, 128), f32),
    ((8, FEAT, 128), f32),
    ((2, FEAT, WIDE), f32),
    ((2,) + FLAT, jnp.int32),
    ((2,) + FLAT, jnp.int32),
)
REAR = (BIG, BIG, BIG, FLAT, FLAT, SUMS[:1] + FLAT, FLAT, SUMS)
REAR = REAR + ((HALF, 8, WIDE), (2, 72, 128), (8, WIDE))
REAR = tuple((shape, f32) for shape in REAR)
RESULT = (
    jax.ShapeDtypeStruct((3, 3, 4, 128), f32),
    jax.ShapeDtypeStruct((8, WIDE), f32),
)


def in_vmem(shapes):
    return [pltpu.VMEM(shape, dtype) for shape, dtype in shapes]


def call(kernel, out_shape, scratch, micros, mib):
    return pl.pallas_call(
        kernel,
        out_shape=out_shape,
        scratch_shapes=scratch,
        compiler_params=pltpu.CompilerParams(vmem_limit_bytes=mib * 2**20),
        cost_estimate=pl.CostEstimate(
            flops=micros * 1_000_000_000, bytes_accessed=2_000_000, transcendentals=2_000_000
        ),
    )


def shaped(shapes):
    return [jax.ShapeDtypeStruct(shape, dtype) for shape, dtype in shapes]


def run_early(*given):
    return call(early, shaped(EARLY), [], 2, 16)(*given)


def run_front(which, *given):
    scratch = in_vmem(TABLE + STEPS[:2])
    return call(functools.partial(opening, which), shaped(KEPT), scratch, 5, 16)(*given)


def run_rear(which, *given):
    return call(functools.partial(rear, ALONE, which), RESULT, in_vmem(STEPS + REAR), 20, 24)(*given)


def run_whole(which, *given):
    scratch = in_vmem(KEPT + TABLE + STEPS + REAR)
    return call(functools.partial(whole, which), RESULT, scratch, 12, 28)(*given)


def shifts(axis, along=None):
    size = lax.axis_size(axis)
    up = [(i, (i + 1) % size) for i in range(size)]
    down = [(j, i) for i, j in up]
    if along is None:
        return axis, up, down
    both_ways = ([(a * size + i, b * size + j) for a, b in along for i, j in way] for way in (up, down))
    return ("gx", axis), *both_ways


def exchange(low, high, axis, dim, along=None):
    axes, up, down = shifts(axis, along)
    if lax.axis_size(axis) == 2:
        return lax.ppermute(jnp.concatenate([high, low], axis=dim), axes, up)
    parts = [lax.ppermute(high, axes, up), lax.ppermute(low, axes, down)]
    return jnp.concatenate(parts, axis=dim)


def neighbours(x, axis, width, along=None):
    axes, up, down = shifts(axis, along)
    if lax.axis_size(axis) == 2:
        return lax.ppermute(x, axes, up)
    below = lax.ppermute(x, axes, up)
    above = lax.ppermute(x, axes, down)
    lane = jnp.arange(x.shape[-1], dtype=jnp.int32)
    return jnp.where(lane % (2 * width) < width, above, below)


def local(
    positions,
    features,
    nbr_index,
    nbr_count,
    bin_counts,
    w_self,
    w_pair,
    w_radial,
    w_tensor,
    w_mix,
    w_out,
):
    cells_x, cells_y = nbr_count.shape[:2]
    cells_z = nbr_count.shape[2] // SLOTS
    lanes = cells_z * SLOTS
    x_index = lax.axis_index("gx")
    y_index = lax.axis_index("gy")
    z_index = lax.axis_index("gz")
    odd = x_index % 2 == 1

    def mirrored(x):
        return jnp.where(odd, x[::-1], x)

    fill = jnp.zeros((ROWS - FEAT - 3,) + positions.shape[1:], f32)
    state = jnp.concatenate([features, positions, fill], axis=0).transpose(1, 0, 2, 3)
    state = mirrored(state.reshape(cells_x, ROWS, cells_y * lanes))
    state_z = neighbours(state, "gz", SLOTS)
    size = lax.axis_size("gx")
    first = [(i, i + 1 - 2 * (i % 2)) for i in range(size)]
    second = [(i, (i - 1 + 2 * (i % 2)) % size) for i in range(size)]
    sides = neighbours(state, "gy", lanes)
    outer = lax.ppermute(state[0], "gx", second)
    inner = lax.ppermute(jnp.stack([state[1], sides[1]]), "gx", first)
    sides_z = neighbours(sides, "gz", SLOTS)
    sides_z, nbr_index, nbr_count, bin_counts = lax.optimization_barrier(
        (sides_z, nbr_index, nbr_count, bin_counts)
    )
    own_counts = lax.dynamic_slice(
        bin_counts,
        (x_index * cells_x, y_index * cells_y, z_index * cells_z),
        (cells_x, cells_y, cells_z),
    )
    slot = jnp.arange(lanes, dtype=jnp.int32) % SLOTS
    limit = jnp.where(slot < jnp.repeat(own_counts, SLOTS, axis=2), nbr_count, 0)
    limit = mirrored(limit) + MIRRORED * odd.astype(jnp.int32)
    limit = jnp.broadcast_to(limit[:, :, None, :], (cells_x, cells_y, 2, lanes))
    limit = limit.reshape(cells_x, 1, WIDE)
    codes = nbr_index.reshape(2, HALF, cells_x, cells_y, lanes)
    codes = mirrored(codes.transpose(2, 1, 3, 0, 4).reshape(cells_x, HALF, WIDE))
    outer, codes, limit = lax.optimization_barrier((outer, codes, limit))
    out_row = w_out[None]
    weights = (w_self, w_pair, w_radial, w_tensor, w_mix.T, out_row)
    merged, *decoded = run_early(state, sides, state_z, sides_z, codes, limit, *weights)
    inner, merged = lax.optimization_barrier((inner, merged))
    inner_z = neighbours(inner, "gz", SLOTS)
    outer_own = jnp.stack([outer, neighbours(outer, "gz", SLOTS)])
    outer_sides = neighbours(outer_own, "gy", lanes)

    kept = run_front(1, inner, inner_z, limit, merged, *decoded)
    late_limit, kept = lax.optimization_barrier((limit, kept))
    grad0, energy0 = run_whole(0, outer_own, outer_sides, late_limit, merged, *decoded, out_row)
    back0 = lax.ppermute(grad0[0], "gx", second)
    grad1, energy1 = run_rear(1, merged, out_row, *decoded[3:], grad0, *kept)
    grad1, back0 = lax.optimization_barrier((grad1, back0))
    grad = grad1[:2] + jnp.stack([back0, jnp.zeros_like(back0)])
    back_y = exchange(grad[:, :, :1], grad[:, :, -1:], "gy", 2)
    back1 = lax.ppermute(grad1[2, :, 1:-1], "gx", first)
    back2 = exchange(grad1[2, :, :1], grad1[2, :, -1:], "gy", 1, first)
    back_y, back1, back2 = lax.optimization_barrier((back_y, back1, back2))
    grad = grad[:, :, 1:-1] + back_y + jnp.stack([jnp.zeros_like(back1), back1 + back2])
    grad = grad[..., SLOTS:-SLOTS] + exchange(grad[..., :SLOTS], grad[..., -SLOTS:], "gz", 3)
    forces = -mirrored(grad).transpose(1, 0, 2, 3)
    energies = mirrored(jnp.stack([energy0[0], energy1[0]]))
    energies = energies.reshape(cells_x, cells_y, 2, lanes)[:, :, 0]
    return forces, energies


def solution(mesh):
    return jax.shard_map(
        local,
        mesh=mesh,
        in_specs=(
            P(None, ("rep", "gx"), "gy", "gz"),
            P(None, ("rep", "gx"), "gy", "gz"),
            P(None, ("rep", "gx"), "gy", "gz"),
            P(("rep", "gx"), "gy", "gz"),
            P("rep", None, None),
            P(),
            P(),
            P(),
            P(),
            P(),
            P(),
        ),
        out_specs=(P(None, ("rep", "gx"), "gy", "gz"), P(("rep", "gx"), "gy", "gz")),
        check_vma=False,
    )
```

```python
import functools

import jax
import jax.numpy as jnp
from jax import lax
from jax.experimental import pallas as pl
from jax.experimental.pallas import tpu as pltpu
from jax.sharding import PartitionSpec as P

SLOTS = 32
cell_side = 6.0
cutoff = 6.0
soften = 0.25
env_norm = 0.25
root2 = 2.0**0.5
f32 = jnp.float32
bf16 = jnp.bfloat16
HALF = 24
WIDE = 256
FEAT = 64
ROWS = 72
BASIS = 8
MIRRORED = 64
SPACING = cutoff / (BASIS - 1)
STEP = 8
ALONE = ((8, 1), (8, 1), (8, 1))
TOGETHER = ((3, 3), (3, 3), (8, 1))

U, Q, ENV, DIST, INV, VEC, DENV, GEO = 0, 3, 9, 10, 11, 12, 15, 16


def halves(x):
    hi = x.astype(bf16)
    return hi, (x - hi.astype(f32)).astype(bf16)


def stacked(x):
    hi, lo = halves(x)
    return jnp.concatenate([hi, lo, hi], axis=0)


def stacked_left(w):
    hi, lo = halves(w)
    return jnp.concatenate([hi, hi, lo], axis=1)


def dot(a, b):
    return jnp.dot(a, b, preferred_element_type=f32)


def small_stack(x):
    hi, lo = halves(x)
    hi, lo = hi.astype(f32), lo.astype(f32)
    return jnp.concatenate([hi, lo, hi, jnp.zeros_like(hi)], axis=0)


def sigmoid(x):
    return 0.5 + 0.5 * jnp.tanh(0.5 * x)


W_A, W_B, W_C, W_D, W_E, W_P, W_S, W_R, W_END = 0, 144, 208, 336, 400, 416, 480, 544, 608


def pipeline(stages, plan, last=None):
    group, unroll = plan
    groups, depth = HALF // group, len(stages)

    def step(t, first, stop):
        for k in range(stop - 1, first - 1, -1):
            start = (t - k) * group
            for i in range(group):
                stages[k](start + i, i)
            if k == depth - 1 and last is not None:
                last(start, group)

    for t in range(depth - 1):
        step(t, 0, t + 1)
    pl.loop(depth - 1, groups, unroll=unroll)(lambda t: step(t, 0, depth))
    for t in range(groups, groups + depth - 1):
        step(t, t - groups + 1, depth)


def one_hot(index, size):
    rows = lax.broadcasted_iota(jnp.int16, (size, index.shape[1]), 0)
    return jnp.where(rows == index.astype(jnp.int16), jnp.ones((), bf16), jnp.zeros((), bf16))


def basis(dist):
    level = lax.broadcasted_iota(jnp.int32, (BASIS, 1), 0).astype(f32)
    x = dist / SPACING - level
    return x, jnp.exp(-x * x)


def lane_row():
    return lax.broadcasted_iota(jnp.int32, (1, 128), 1)


def fold_sides(x):
    return jnp.concatenate(
        [x[:, c : c + 128] + pltpu.roll(x[:, c : c + 128], 64, 1) for c in (0, 128)], axis=1
    )


def prepare(w_self, w_pair, w_radial, w_tensor, mix_t, w_out, merged):
    tensor, mix, out_row = w_tensor[...], mix_t[...].T, w_out[...]
    parts = (
        jnp.concatenate(
            [tensor.T, mix_t[:, :FEAT], jnp.broadcast_to(out_row, (16, FEAT))], axis=0
        ),
        mix_t[:, FEAT:],
        mix * out_row,
        tensor,
        jnp.concatenate([w_radial[...], jnp.zeros_like(w_radial)], axis=0),
        w_pair[...].T,
        w_self[...].T,
    )
    for first, part in zip((W_A, W_B, W_C, W_D, W_E, W_P, W_S), parts):
        merged[first : first + part.shape[0], :] = stacked_left(part)
    hi, lo = halves(w_radial[...])
    hi, lo = hi.astype(f32), lo.astype(f32)
    rows = jnp.concatenate([hi, hi, lo, jnp.zeros((168, FEAT), f32)], axis=0)
    merged[W_R:W_END, :] = rows.T.astype(bf16)


def joined_column(yc, own, sides, own_z, sides_z):
    mine, theirs = (sides, sides_z) if yc in (0, 3) else (own, own_z)
    first, second = (96, 32) if yc in (0, 2) else (32, 96)
    lanes = lane_row()
    inside = (lanes >= 32) & (lanes < 96)
    return jnp.where(inside, pltpu.roll(mine[...], first, 1), pltpu.roll(theirs[...], second, 1))


def both(x):
    return jnp.where(lane_row() < 64, pltpu.roll(x, 96, 1), pltpu.roll(x, 32, 1))


def early(
    own,
    sides,
    own_z,
    sides_z,
    codes,
    limits,
    w_self,
    w_pair,
    w_radial,
    w_tensor,
    mix_t,
    w_out,
    merged,
    columns,
    pair,
    self_t,
    lane_i,
    col_i,
):
    prepare(w_self, w_pair, w_radial, w_tensor, mix_t, w_out, merged)
    for x in range(2):
        blocks = [block.at[x] for block in (own, sides, own_z, sides_z)]
        for yc in range(4):
            columns[4 * x + yc] = joined_column(yc, *blocks)
        rows = jnp.concatenate([columns[4 * x + yc, :FEAT, :] for yc in range(4)], axis=1)
        terms = dot(merged[W_P:W_S, :], stacked(rows))
        self_terms = dot(merged[W_S:W_R, :], stacked(rows[:, 128:384]))
        for yc in range(4):
            pair[4 * x + yc] = terms[:, 128 * yc : 128 * yc + 128]
        for y in range(2):
            self_t[x, :, 128 * y : 128 * y + 128] = both(self_terms[:, 128 * y : 128 * y + 128])
        code = codes[x]
        offset = code >> 5
        plane = (offset * 43) >> 7
        dz = offset - 3 * plane
        dx = (offset * 57) >> 9
        lane256 = lax.broadcasted_iota(jnp.int32, (HALF, WIDE), 1)
        lane_i[x] = ((((lane256 >> 5) & 1) + dz) << 5) + (code & 31)
        col_i[x] = plane + jnp.where(limits[x] >= MIRRORED, 6 - 6 * dx, 0)


def front(
    plan,
    which,
    ghost_own,
    ghost_sides,
    ghost_own_z,
    ghost_sides_z,
    limit,
    merged,
    columns,
    pair,
    self_t,
    lane_i,
    col_i,
    act,
    slope,
    tens,
    mix0,
    v_acc,
    e_row,
    geo,
    table,
    ghost,
    step_a,
    step_b,
):
    w_a, w_p = merged.at[W_A:W_B], merged.at[W_P:W_S]
    w_r = merged.at[W_R:W_END, 0 : 4 * BASIS]
    self_t, lane_i, col_i = self_t.at[which], lane_i.at[which], col_i.at[which]
    far_layer = 0 if which == 0 else 2
    near_first = 3 if which == 0 else 0

    def source(dx, yc):
        return ghost.at[yc] if dx == far_layer else columns.at[4 * (dx - 1 + which) + yc]

    for yc in range(4):
        ghost[yc] = joined_column(yc, ghost_own, ghost_sides, ghost_own_z, ghost_sides_z)

    rows = jnp.concatenate([source(far_layer, yc)[:FEAT, :] for yc in range(4)], axis=1)
    hi, lo = halves(dot(w_p[...], stacked(rows)))
    table[:FEAT] = hi
    table[FEAT:] = lo

    lane256 = lax.broadcasted_iota(jnp.int32, (HALF, WIDE), 1)
    column = col_i[...]
    mirrored = (column * 11) >> 5
    limits = limit[which]
    dx = jnp.where(limits >= MIRRORED, 2 - mirrored, mirrored)
    dy = column - 3 * mirrored
    dz = (lane_i[...] >> 5) - ((lane256 >> 5) & 1)
    rank = lax.broadcasted_iota(jnp.int32, (HALF, WIDE), 0) + HALF * ((lane256 >> 6) & 1)
    mask = (rank < (limits & (MIRRORED - 1))).astype(f32)

    steps = (dx, dy, dz)
    vec = []
    for d in range(3):
        found = []
        for y in range(2):
            own = both(source(1, 1 + y)[FEAT + d : FEAT + d + 1, :])
            parts = []
            for j in range(HALF // 8):
                where = (slice(8 * j, 8 * j + 8), slice(128 * y, 128 * y + 128))
                lane, col = lane_i[where], col_i[where]
                acc = None
                for c in range(9):
                    row = source(c // 3, y + c % 3)[FEAT + d : FEAT + d + 1, :]
                    value = jnp.take_along_axis(
                        jnp.broadcast_to(row, (8, 128)), lane, axis=1, mode="promise_in_bounds"
                    )
                    acc = value if c == 0 else jnp.where(col == c, value, acc)
                parts.append(acc)
            found.append(jnp.concatenate(parts, axis=0) - own)
        vec.append(
            jnp.concatenate(found, axis=1) + cell_side * (steps[d] - 1).astype(f32)
        )
    squared = vec[0] * vec[0] + vec[1] * vec[1] + vec[2] * vec[2] + soften
    dist = jnp.sqrt(squared)
    inv = 1.0 / dist
    u = [v * inv for v in vec]
    taper = jnp.maximum(1.0 - squared / (cutoff * cutoff), 0.0)
    for d in range(3):
        geo[U + d] = u[d]
        geo[VEC + d] = vec[d]
        geo[Q + d] = u[d] * u[d] - 1.0 / 3.0
    geo[Q + 3] = root2 * u[0] * u[1]
    geo[Q + 4] = root2 * u[0] * u[2]
    geo[Q + 5] = root2 * u[1] * u[2]
    geo[ENV] = taper * taper * mask
    geo[DENV] = taper * mask * (-2.0 / (cutoff * cutoff))
    geo[DIST] = dist
    geo[INV] = inv

    def row(k, s):
        return geo[k, pl.ds(s, 1), :]

    v_acc[...] = jnp.zeros_like(v_acc)

    def gathered(s):
        lane_s = lane_i[pl.ds(s, 1), :]
        col_s = col_i[pl.ds(s, 1), :]
        far_col = col_s - 3 * far_layer + (lax.broadcasted_iota(jnp.int32, (1, WIDE), 1) >> 7)
        is_far = (col_s < 3) if which == 0 else (col_s >= 6)
        spots = jnp.where(is_far, (far_col << 7) + lane_s, -1)
        sides = []
        for y in range(2):
            lane = jnp.broadcast_to(lane_s[:, 128 * y : 128 * y + 128], (8, 128))
            col = jnp.broadcast_to(col_s[:, 128 * y : 128 * y + 128], (8, 128))
            masks = [col == c + near_first for c in range(6)]
            near = (col >= 3) if which == 0 else (col < 6)
            groups = []
            for g in range(FEAT // 8):
                acc = None
                for c in range(6):
                    value = jnp.take_along_axis(
                        pair[(c // 3) * 4 + y + c % 3, 8 * g : 8 * g + 8, :],
                        lane,
                        axis=1,
                        mode="promise_in_bounds",
                    )
                    acc = value if c == 0 else jnp.where(masks[c], value, acc)
                groups.append(jnp.where(near, acc, 0.0))
            sides.append(jnp.concatenate(groups, axis=0))
        far = dot(table[...], one_hot(spots, 512))
        return jnp.concatenate(sides, axis=1) + (far[:FEAT] + far[FEAT:])

    def forward_a(s, i):
        _, waves = basis(row(DIST, s))
        step_a[i] = dot(w_r[...], small_stack(waves).astype(bf16)) + (self_t[...] + gathered(s))

    def forward_b(s, i):
        z = step_a[i]
        sg = sigmoid(z)
        silu = z * sg
        env = row(ENV, s)
        act[s] = silu
        slope[s] = (sg + silu * (1.0 - sg)) * env
        both_t = dot(w_a[...], stacked(silu * env))
        tens[s] = both_t[:FEAT]
        mix0[s] = both_t[FEAT : 2 * FEAT]
        e_row[pl.ds(s, 1), :] = both_t[2 * FEAT : 2 * FEAT + 1]

    def forward_c(s, i):
        pass

    def forward_sum(first, group):
        for k in range(9):
            part = slice(0, 32) if k < 3 else slice(32, 64)
            total = v_acc[k]
            for i in range(group):
                total += tens[first + i, part] * row(k, first + i)
            v_acc[k] = total

    pipeline((forward_a, forward_b, forward_c), plan[0], forward_sum)

    for k in range(9):
        v_acc[k] = env_norm * fold_sides(v_acc[k])


def rear(
    plan,
    which,
    merged,
    out_row,
    lane_i,
    col_i,
    added,
    act,
    slope,
    tens,
    mix0,
    v_acc,
    e_row,
    geo,
    out,
    energy,
    step_a,
    step_b,
    step_c,
    prod,
    back,
    resid,
    m_row,
    d_row,
    du_row,
    dr_row,
    dv_acc,
    g_row,
    s_acc,
    own_sum,
):
    lane_i, col_i = lane_i.at[which], col_i.at[which]
    w_b, w_c = merged.at[W_B:W_C], merged.at[W_C:W_D]
    w_d, w_e = merged.at[W_D:W_E], merged.at[W_E:W_P]
    lanes = lane_row()

    def row(k, s):
        return geo[k, pl.ds(s, 1), :]

    dv_acc[...] = jnp.zeros_like(dv_acc)
    col_w = jnp.broadcast_to(out_row[...], (128, FEAT)).T
    col_w = jnp.concatenate([col_w, col_w], axis=1)

    def middle_a(s, i):
        vec_in = v_acc[0] * row(0, s)
        for k in range(1, 3):
            vec_in += v_acc[k] * row(k, s)
        ten_in = v_acc[3] * row(3, s)
        for k in range(4, 9):
            ten_in += v_acc[k] * row(k, s)
        inner = jnp.concatenate([vec_in, ten_in], axis=0)
        back[s] = inner
        step_a[i] = mix0[s] + dot(w_b[...], stacked(tens[s] * inner))

    def middle_b(s, i):
        mixture = step_a[i]
        sg = sigmoid(mixture)
        silu = mixture * sg
        m_row[pl.ds(s, 1), :] = jnp.sum(col_w * silu, axis=0, keepdims=True)
        grad = (sg + silu * (1.0 - sg)) * row(ENV, s)
        pulled = dot(w_c[...], stacked(grad))
        resid[s] = pulled[:FEAT] + col_w
        step_c[i] = pulled[FEAT:]

    def middle_c(s, i):
        dvt = step_c[i]
        back[s] = dvt * back[s]
        p = dvt * tens[s]
        prod[s] = p

    def middle_sum(first, group):
        for k in range(9):
            part = slice(0, 32) if k < 3 else slice(32, 64)
            total = dv_acc[k]
            for i in range(group):
                total += prod[first + i, part] * row(k, first + i)
            dv_acc[k] = total

    pipeline((middle_a, middle_b, middle_c), plan[1], middle_sum)

    for k in range(9):
        dv_acc[k] = env_norm * fold_sides(dv_acc[k])

    def backward_a(s, i):
        t = tens[s]
        p = prod[s]
        dt = back[s]
        vec_part, ten_part = dt[:32], dt[32:]
        for k in range(9):
            half = slice(0, 32) if k < 3 else slice(32, 64)
            moved = dv_acc[k]
            if k < 3:
                vec_part += moved * row(k, s)
            else:
                ten_part += moved * row(k, s)
            du_row[k, pl.ds(s, 1), :] = jnp.sum(
                p[half] * v_acc[k] + t[half] * moved, axis=0, keepdims=True
            )
        step_a[i] = resid[s] + dot(
            w_d[...], stacked(jnp.concatenate([vec_part, ten_part], axis=0))
        )

    def backward_b(s, i):
        dl = step_a[i]
        d_row[pl.ds(s, 1), :] = jnp.sum(dl * act[s], axis=0, keepdims=True)
        step_b[i, :16] = dot(w_e[...], stacked(dl * slope[s]))

    def backward_c(s, i):
        x, waves = basis(row(DIST, s))
        dr_row[pl.ds(s, 1), :] = jnp.sum(step_b[i, :8] * waves * x, axis=0, keepdims=True)

    pipeline((backward_a, backward_b, backward_c), plan[2])

    env, m_sum = geo[ENV], m_row[...]
    values = jnp.sum(e_row[...] + env * m_sum, axis=0, keepdims=True)
    energy[...] = jnp.broadcast_to(fold_sides(values), energy.shape)
    u = [geo[U + d] for d in range(3)]
    du = [du_row[d] for d in range(3)]
    dq = [du_row[3 + k] for k in range(6)]
    cross = ((0, 1, 3), (0, 2, 4), (1, 2, 5))
    du = [du[d] + 2.0 * u[d] * dq[d] for d in range(3)]
    for a, b, k in cross:
        du[a] = du[a] + root2 * u[b] * dq[k]
        du[b] = du[b] + root2 * u[a] * dq[k]
    inv = geo[INV]
    along = du[0] * u[0] + du[1] * u[1] + du[2] * u[2]
    dr = dr_row[...] * (-2.0 / SPACING) - along * inv
    ds = 2.0 * geo[DENV] * (d_row[...] + m_sum) + dr * inv
    zero = jnp.zeros((HALF, WIDE), f32)
    for d in range(3):
        g = du[d] * inv + geo[VEC + d] * ds
        hi, lo = halves(g)
        g_row[:, d, :] = hi.astype(f32)
        g_row[:, 3 + d, :] = lo.astype(f32)
        own = fold_sides(jnp.sum(g, axis=0, keepdims=True))
        own_sum[d : d + 1, :] = own
    g_row[:, 6, :] = zero
    g_row[:, 7, :] = zero

    s_acc[...] = jnp.zeros_like(s_acc)

    @pl.loop(0, HALF // 4, unroll=6)
    def scatter(q):
        for y in range(2):
            side = slice(128 * y, 128 * y + 128)
            left, right = [], []
            for i in range(4):
                s = 4 * q + i
                lane = lane_i[pl.ds(s, 1), :][:, side]
                col = jnp.broadcast_to(col_i[pl.ds(s, 1), :][:, side], (8, 128))
                tile = g_row[s, :, side]
                left.append(
                    jnp.concatenate(
                        [jnp.where(col == c, tile, 0.0) for c in range(9)], axis=0
                    ).astype(bf16)
                )
                right.append(one_hot(lane, 128))
            s_acc[y] += lax.dot_general(
                jnp.concatenate(left, axis=1),
                jnp.concatenate(right, axis=1),
                (((1,), (1,)), ((), ())),
                preferred_element_type=f32,
            )

    if added is None:
        out[...] = jnp.zeros_like(out)
    else:
        out[0:2] = added[1:3]
        out[2:3] = jnp.zeros_like(out[2:3])
    for y in range(2):
        for c in range(9):
            tile = s_acc[y, 8 * c : 8 * c + 8, :]
            for d in range(3):
                out[c // 3, d, y + c % 3 : y + c % 3 + 1, :] += tile[d : d + 1] + tile[3 + d : 4 + d]
        own = pltpu.roll(own_sum[:, 128 * y : 128 * y + 128], 32, 1)
        kept = jnp.where((lanes >= 32) & (lanes < 96), own, 0.0)
        for d in range(3):
            out[1, d, 1 + y : 2 + y, :] -= kept[d : d + 1]


def whole(which, *refs):
    (own, sides), given, out_row, out, rest = refs[:2], refs[2:9], refs[9], refs[10:12], refs[12:]
    kept, tables, steps, rest = rest[:7], rest[7:9], rest[9:12], rest[12:]
    ghost = (own.at[0], sides.at[0], own.at[1], sides.at[1])
    front(TOGETHER, which, *ghost, *given[:1], *given[1:], *kept, *tables, *steps[:2])
    rear(TOGETHER, which, given[1], out_row, *given[5:7], None, *kept, *out, *steps, *rest)


def opening(which, ghost, ghost_z, *refs):
    blocks = (ghost.at[0], ghost.at[1], ghost_z.at[0], ghost_z.at[1])
    front(ALONE, which, *blocks, *refs)


BIG = (HALF, FEAT, WIDE)
FLAT = (HALF, WIDE)
SUMS = (9, 32, WIDE)
KEPT = (
    (BIG, f32),
    (BIG, f32),
    (BIG, f32),
    (BIG, f32),
    (SUMS, f32),
    (FLAT, f32),
    ((GEO, HALF, WIDE), f32),
)
STEPS = tuple(((STEP, rows, WIDE), f32) for rows in (FEAT, 2 * FEAT + 16, FEAT))
TABLE = (((2 * FEAT, 4 * 128), bf16), ((4, ROWS, 128), f32))
EARLY = (
    ((W_END, 3 * FEAT), bf16),
    ((8, ROWS, 128), f32),
    ((8, FEAT, 128), f32),
    ((2, FEAT, WIDE), f32),
    ((2,) + FLAT, jnp.int32),
    ((2,) + FLAT, jnp.int32),
)
REAR = (BIG, BIG, BIG, FLAT, FLAT, SUMS[:1] + FLAT, FLAT, SUMS)
REAR = REAR + ((HALF, 8, WIDE), (2, 72, 128), (8, WIDE))
REAR = tuple((shape, f32) for shape in REAR)
RESULT = (
    jax.ShapeDtypeStruct((3, 3, 4, 128), f32),
    jax.ShapeDtypeStruct((8, WIDE), f32),
)


def in_vmem(shapes):
    return [pltpu.VMEM(shape, dtype) for shape, dtype in shapes]


def call(kernel, out_shape, scratch, micros, mib):
    return pl.pallas_call(
        kernel,
        out_shape=out_shape,
        scratch_shapes=scratch,
        compiler_params=pltpu.CompilerParams(vmem_limit_bytes=mib * 2**20),
        cost_estimate=pl.CostEstimate(
            flops=micros * 1_000_000_000, bytes_accessed=2_000_000, transcendentals=2_000_000
        ),
    )


def shaped(shapes):
    return [jax.ShapeDtypeStruct(shape, dtype) for shape, dtype in shapes]


def run_early(*given):
    return call(early, shaped(EARLY), [], 2, 16)(*given)


def run_front(which, *given):
    scratch = in_vmem(TABLE + STEPS[:2])
    return call(functools.partial(opening, which), shaped(KEPT), scratch, 5, 16)(*given)


def run_rear(which, *given):
    return call(functools.partial(rear, ALONE, which), RESULT, in_vmem(STEPS + REAR), 20, 24)(*given)


def run_whole(which, *given):
    scratch = in_vmem(KEPT + TABLE + STEPS + REAR)
    return call(functools.partial(whole, which), RESULT, scratch, 12, 28)(*given)


def shifts(axis, along=None):
    size = lax.axis_size(axis)
    up = [(i, (i + 1) % size) for i in range(size)]
    down = [(j, i) for i, j in up]
    if along is None:
        return axis, up, down
    both_ways = ([(a * size + i, b * size + j) for a, b in along for i, j in way] for way in (up, down))
    return ("gx", axis), *both_ways


def exchange(low, high, axis, dim, along=None):
    axes, up, down = shifts(axis, along)
    if lax.axis_size(axis) == 2:
        return lax.ppermute(jnp.concatenate([high, low], axis=dim), axes, up)
    parts = [lax.ppermute(high, axes, up), lax.ppermute(low, axes, down)]
    return jnp.concatenate(parts, axis=dim)


def neighbours(x, axis, width, along=None):
    axes, up, down = shifts(axis, along)
    if lax.axis_size(axis) == 2:
        return lax.ppermute(x, axes, up)
    below = lax.ppermute(x, axes, up)
    above = lax.ppermute(x, axes, down)
    lane = jnp.arange(x.shape[-1], dtype=jnp.int32)
    return jnp.where(lane % (2 * width) < width, above, below)


def local(
    positions,
    features,
    nbr_index,
    nbr_count,
    bin_counts,
    w_self,
    w_pair,
    w_radial,
    w_tensor,
    w_mix,
    w_out,
):
    cells_x, cells_y = nbr_count.shape[:2]
    cells_z = nbr_count.shape[2] // SLOTS
    lanes = cells_z * SLOTS
    x_index = lax.axis_index("gx")
    y_index = lax.axis_index("gy")
    z_index = lax.axis_index("gz")
    odd = x_index % 2 == 1

    def mirrored(x):
        return jnp.where(odd, x[::-1], x)

    fill = jnp.zeros((ROWS - FEAT - 3,) + positions.shape[1:], f32)
    state = jnp.concatenate([features, positions, fill], axis=0).transpose(1, 0, 2, 3)
    state = mirrored(state.reshape(cells_x, ROWS, cells_y * lanes))
    state_z = neighbours(state, "gz", SLOTS)
    size = lax.axis_size("gx")
    first = [(i, i + 1 - 2 * (i % 2)) for i in range(size)]
    second = [(i, (i - 1 + 2 * (i % 2)) % size) for i in range(size)]
    sides = neighbours(state, "gy", lanes)
    outer = lax.ppermute(state[0], "gx", second)
    inner = lax.ppermute(jnp.stack([state[1], sides[1]]), "gx", first)
    sides_z = neighbours(sides, "gz", SLOTS)
    sides_z, nbr_index, nbr_count, bin_counts = lax.optimization_barrier(
        (sides_z, nbr_index, nbr_count, bin_counts)
    )
    own_counts = lax.dynamic_slice(
        bin_counts,
        (x_index * cells_x, y_index * cells_y, z_index * cells_z),
        (cells_x, cells_y, cells_z),
    )
    slot = jnp.arange(lanes, dtype=jnp.int32) % SLOTS
    limit = jnp.where(slot < jnp.repeat(own_counts, SLOTS, axis=2), nbr_count, 0)
    limit = mirrored(limit) + MIRRORED * odd.astype(jnp.int32)
    limit = jnp.broadcast_to(limit[:, :, None, :], (cells_x, cells_y, 2, lanes))
    limit = limit.reshape(cells_x, 1, WIDE)
    codes = nbr_index.reshape(2, HALF, cells_x, cells_y, lanes)
    codes = mirrored(codes.transpose(2, 1, 3, 0, 4).reshape(cells_x, HALF, WIDE))
    outer, codes, limit = lax.optimization_barrier((outer, codes, limit))
    out_row = w_out[None]
    weights = (w_self, w_pair, w_radial, w_tensor, w_mix.T, out_row)
    merged, *decoded = run_early(state, sides, state_z, sides_z, codes, limit, *weights)
    inner, merged = lax.optimization_barrier((inner, merged))
    inner_z = neighbours(inner, "gz", SLOTS)
    outer_own = jnp.stack([outer, neighbours(outer, "gz", SLOTS)])
    outer_sides = neighbours(outer_own, "gy", lanes)

    kept = run_front(1, inner, inner_z, limit, merged, *decoded)
    late_limit, kept = lax.optimization_barrier((limit, kept))
    grad0, energy0 = run_whole(0, outer_own, outer_sides, late_limit, merged, *decoded, out_row)
    back0 = lax.ppermute(grad0[0], "gx", second)
    grad1, energy1 = run_rear(1, merged, out_row, *decoded[3:], grad0, *kept)
    grad1, back0 = lax.optimization_barrier((grad1, back0))
    grad = grad1[:2] + jnp.stack([back0, jnp.zeros_like(back0)])
    back_y = exchange(grad[:, :, :1], grad[:, :, -1:], "gy", 2)
    back1 = lax.ppermute(grad1[2, :, 1:-1], "gx", first)
    back2 = exchange(grad1[2, :, :1], grad1[2, :, -1:], "gy", 1, first)
    back_y, back1, back2 = lax.optimization_barrier((back_y, back1, back2))
    grad = grad[:, :, 1:-1] + back_y + jnp.stack([jnp.zeros_like(back1), back1 + back2])
    grad = grad[..., SLOTS:-SLOTS] + exchange(grad[..., :SLOTS], grad[..., -SLOTS:], "gz", 3)
    forces = -mirrored(grad).transpose(1, 0, 2, 3)
    energies = mirrored(jnp.stack([energy0[0], energy1[0]]))
    energies = energies.reshape(cells_x, cells_y, 2, lanes)[:, :, 0]
    return forces, energies


def solution(mesh):
    return jax.shard_map(
        local,
        mesh=mesh,
        in_specs=(
            P(None, ("rep", "gx"), "gy", "gz"),
            P(None, ("rep", "gx"), "gy", "gz"),
            P(None, ("rep", "gx"), "gy", "gz"),
            P(("rep", "gx"), "gy", "gz"),
            P("rep", None, None),
            P(),
            P(),
            P(),
            P(),
            P(),
            P(),
        ),
        out_specs=(P(None, ("rep", "gx"), "gy", "gz"), P(("rep", "gx"), "gy", "gz")),
        check_vma=False,
    )
```
